32 devices in a mesh: groups: 2 (over y), gx: 4 (over z), gy: 4 (over x, core).
Axes of the slice: x: 2, y: 2, z: 4, core: 2. Of those that a mesh axis runs over, the one named last changes fastest.
Arguments:
- tokens: bfloat16 [128, 8192], P(('groups', 'gx'), 'gy'), parts along dimension 0, may hold values from -220 to 220
- norm_gain: float32 [8192], P('gy'), may hold values from 0.85 to 12
- w_query: bfloat16 [8192, 8192], P('gy', 'gx'), may hold values from -0.0625 to 0.0625
- keyvalue_weight: bfloat16 [8192, 2048], P('gy', 'gx'), may hold values from -0.0625 to 0.0625
- w_out: bfloat16 [8192, 8192], P('gy', 'gx'), may hold values from -0.0625 to 0.0625
- segment_ids: int32 [8, 16], P(('groups', 'gx')), parts along dimension 0, may hold values from 0 to 2, never falling along the last dimension, each value on 1 to 8 neighbouring positions
Outputs:
- attn_out: bfloat16 [128, 8192], P(('groups', 'gy'), 'gx'), parts along dimension 0
The draws below stay inside these ranges and needn't reach their ends.
There are 2 independent parts, one for each index of `groups`. The reference program is written for one: setup_inputs(seed, part) draws one part's arguments, and reference() takes and returns one part's arrays. A program takes and returns all parts, laid end to end along the dimension named above; an argument that names none is the same for every part. Nothing has to cross between parts.
Inputs may be any that keep to these rules, and one draw needn't show every extreme that they name: `segment_ids`: in each request the ids never fall along the rows; every id of 0 to 2 covers 1 to 8 consecutive rows, some id exactly 8.
All inputs are finite; a program needn't handle non-finite values.
Results may differ from the reference program's by a relative error of at most 0.00405.
The reference program's roundings to bfloat16 on the way count: a program that leaves them out, or rounds other values in their place, can miss the bound.
Values may be sent and summed in bfloat16 or wider, within the bound.
A program may use at most 64 MiB of HBM per device.

```python
import math
import jax
import jax.numpy as jnp
import numpy as np
from jax import lax

MODEL_WIDTH = 8192
QUERY_HEADS = 64
KEYVALUE_HEADS = 8
HEAD_WIDTH = 128
REQUEST_ROWS = 16
SEGS = 3
REQS = 4
TOTAL_ROWS = 64
SEG_MOST = 8


def draw_tokens(key, part):
    key = jax.random.fold_in(key, 11)
    row_key, column_key, base_key = jax.random.split(key, 3)
    row_scale = jnp.exp(jax.random.uniform(row_key, (TOTAL_ROWS, 1), minval=0.0, maxval=math.log(10.0)))
    base_values = jnp.clip(jax.random.normal(base_key, (TOTAL_ROWS, MODEL_WIDTH)), -4.0, 4.0)
    column_ramp = jnp.exp(jnp.arange(MODEL_WIDTH, dtype=jnp.float32) * (0.5 * math.log(3.0) / MODEL_WIDTH))
    column_scale = column_ramp[None, :] * jnp.exp(jax.random.uniform(column_key, (1, MODEL_WIDTH), minval=-1.15, maxval=1.15))
    return (base_values * row_scale * column_scale).astype(jnp.bfloat16)


def draw_norm_gain(key, part):
    key = jax.random.fold_in(key, 23)
    return (1.0 + 0.15 * jax.random.uniform(key, (MODEL_WIDTH,), minval=-1.0, maxval=1.0)).astype(jnp.float32)


def shard_levels(stream_key, dims, cuts, least, largest):
    gain, own = 1.0, jax.random.fold_in(stream_key, 6)
    for axis_at, blocks in cuts:
        draws = jnp.exp(jax.random.uniform(jax.random.fold_in(own, axis_at), (blocks,), jnp.float32, least / len(cuts), largest / len(cuts)))
        gain = gain * jnp.repeat(draws, dims[axis_at] // blocks).reshape([-1 if axis == axis_at else 1 for axis in range(len(dims))])
    return gain


def split_up(number_of, total, bound, slope):
    weights = [(1 << 20) // math.isqrt(grade ** slope) + 1 for grade in range(2, number_of + 1)]
    spare, holding = total - bound - (number_of - 1), [1] * (number_of - 1)
    while spare > 0:
        candidates = [i for i in range(number_of - 1) if holding[i] < bound]
        pool, budget = sum([weights[i] for i in candidates]), spare
        for i in candidates:
            more = min(bound - holding[i], max(1, budget * weights[i] // pool), spare)
            holding[i] = holding[i] + more
            spare = spare - more
    return np.array([bound] + holding)


def ragged(key, amount, total, reach, lean):
    if amount == 2:
        one = jax.random.randint(key, (), max(1, total - reach), min(reach, total - 1) + 1)
        return jnp.stack([one, total - one])
    tallies = jnp.asarray(split_up(amount, total, reach, lean), jnp.int32)
    pairs = (amount - 1) // 2
    source_of, taker = tallies[1:1 + 2 * pairs:2], tallies[2:2 + 2 * pairs:2]
    room = jnp.minimum(source_of - 1, reach - taker)
    passed = jax.random.randint(jax.random.fold_in(key, 1), (pairs,), 0, 1 << 20) % (room + 1)
    tallies = tallies.at[1:1 + 2 * pairs:2].set(source_of - passed).at[2:2 + 2 * pairs:2].set(taker + passed)
    return tallies[jax.random.permutation(jax.random.fold_in(key, 2), amount)]


def normal_values(own_key, shape, width, limit, cuts=(), kind=jnp.bfloat16):
    drawn = jax.random.normal(own_key, shape, jnp.float32) * width
    if len(cuts) > 0:
        drawn = shard_levels(own_key, shape, cuts, -0.22, 0.18) * drawn
    return jnp.clip(drawn, min=-limit, max=limit).astype(kind)


def setup_inputs(seed: int = 0, part: int = 0) -> dict:
    arg_keys = jax.random.split(jax.random.key(seed), 7)
    own_keys = jax.random.split(jax.random.fold_in(arg_keys[6], part), 7)
    return {
        "tokens": draw_tokens(jax.random.fold_in(jax.random.fold_in(arg_keys[6], part), 71), part),
        "norm_gain": draw_norm_gain(jax.random.fold_in(arg_keys[6], 71), part),
        "w_query": normal_values(arg_keys[2], (MODEL_WIDTH, QUERY_HEADS * HEAD_WIDTH), MODEL_WIDTH ** -0.5, 0.0625, ((0, 4), (1, 4))),
        "keyvalue_weight": normal_values(arg_keys[3], (MODEL_WIDTH, 2 * KEYVALUE_HEADS * HEAD_WIDTH), MODEL_WIDTH ** -0.5, 0.0625, ((0, 4), (1, 4))),
        "w_out": normal_values(arg_keys[4], (QUERY_HEADS * HEAD_WIDTH, MODEL_WIDTH), (QUERY_HEADS * HEAD_WIDTH) ** -0.5, 0.0625, ((0, 4), (1, 4))),
        "segment_ids": jax.vmap(lambda own: jnp.searchsorted(jnp.cumsum(ragged(own, SEGS, REQUEST_ROWS, SEG_MOST, 1)), jnp.arange(REQUEST_ROWS), side="right"))(jax.random.split(own_keys[5], REQS)).reshape((REQS, REQUEST_ROWS)).astype(jnp.int32),
    }


EPSILON = 1e-05
ROPE_BASE = 500000.0
MASK_VALUE = -1e+30

def row_positions(segments, segment_total):
    bounds = jnp.arange(segment_total + 1, dtype=jnp.int32)
    first_rows = lax.optimization_barrier(jnp.sum((segments[:, None, :] < bounds[None, :, None]).astype(jnp.int32), axis=2)).astype(jnp.int32)
    matches = segments[:, :, None] == bounds[None, None, :segment_total]
    segment_first = lax.optimization_barrier(jnp.sum(jnp.where(matches, first_rows[:, None, :segment_total], 0), axis=2)).astype(jnp.int32)
    context_length = first_rows[:, 1:2]
    row_index = jnp.arange(segments.shape[1], dtype=jnp.int32)[None, :]
    positions = jnp.where(segments == 0, row_index, context_length + row_index - segment_first)
    return positions.astype(jnp.int32).reshape(-1)

def rotate(values, positions):
    half_size = values.shape[-1] // 2
    frequency = ROPE_BASE ** (-2.0 * jnp.arange(half_size, dtype=jnp.float32) / values.shape[-1])
    angle = positions.astype(jnp.float32)[:, None, None] * frequency[None, None, :]
    cosine = jnp.cos(angle)
    sine = jnp.sin(angle)
    first_half = values[..., :half_size]
    second_half = values[..., half_size:]
    return jnp.concatenate([first_half * cosine - second_half * sine, second_half * cosine + first_half * sine], axis=-1)

def request_mask(segments):
    row_index = jnp.arange(segments.shape[0], dtype=jnp.int32)
    causal = row_index[None, :] <= row_index[:, None]
    same_part = (segments[None, :] == segments[:, None]) | (segments[None, :] == 0)
    return causal & same_part

def reference(tokens, norm_gain, w_query, keyvalue_weight, w_out, segment_ids):
    widened = tokens.astype(jnp.float32)
    mean_square = lax.optimization_barrier(jnp.mean(widened * widened, axis=1))
    normalized_input = (widened * lax.rsqrt(mean_square + EPSILON)[:, None] * norm_gain[None, :]).astype(jnp.bfloat16)
    positions = row_positions(segment_ids, SEGS)
    heads_of_query = jnp.dot(normalized_input, w_query, preferred_element_type=jnp.float32).reshape(TOTAL_ROWS, QUERY_HEADS, HEAD_WIDTH)
    heads_of_query = rotate(heads_of_query, positions).astype(jnp.bfloat16)
    keyvalue_pairs = jnp.dot(normalized_input, keyvalue_weight, preferred_element_type=jnp.float32).reshape(TOTAL_ROWS, KEYVALUE_HEADS, 2, HEAD_WIDTH)
    key_heads = rotate(keyvalue_pairs[:, :, 0], positions).astype(jnp.bfloat16)
    value_heads = keyvalue_pairs[:, :, 1].astype(jnp.bfloat16)
    group_width = QUERY_HEADS // KEYVALUE_HEADS
    score_scale = HEAD_WIDTH ** (-0.5)

    def attend(request):
        start_shift = request * REQUEST_ROWS
        query_block = lax.dynamic_slice_in_dim(heads_of_query, start_shift, REQUEST_ROWS, 0).reshape(REQUEST_ROWS, KEYVALUE_HEADS, group_width, HEAD_WIDTH)
        block_keys = lax.dynamic_slice_in_dim(key_heads, start_shift, REQUEST_ROWS, 0)
        block_values = lax.dynamic_slice_in_dim(value_heads, start_shift, REQUEST_ROWS, 0)
        segments = lax.dynamic_slice_in_dim(segment_ids, request, 1, 0)[0]
        visible = request_mask(segments)
        scores = jnp.einsum('rkgd,tkd->kgrt', query_block.astype(jnp.float32), block_keys.astype(jnp.float32), precision=lax.Precision.HIGHEST) * score_scale
        scores = jnp.where(visible[None, None], scores, MASK_VALUE)
        row_top = lax.optimization_barrier(jnp.max(scores, axis=-1, keepdims=True))
        weights = jnp.exp(scores - row_top)
        probabilities = (weights / lax.optimization_barrier(jnp.sum(weights, axis=-1, keepdims=True))).astype(jnp.bfloat16)
        mixed_heads = jnp.einsum('kgrt,tkd->rkgd', probabilities.astype(jnp.float32), block_values.astype(jnp.float32), precision=lax.Precision.HIGHEST)
        return mixed_heads.astype(jnp.bfloat16).reshape(REQUEST_ROWS, QUERY_HEADS * HEAD_WIDTH)
    mixed = lax.map(attend, jnp.arange(REQS, dtype=jnp.int32)).reshape(TOTAL_ROWS, QUERY_HEADS * HEAD_WIDTH)
    return jnp.dot(mixed, w_out, preferred_element_type=jnp.float32).astype(jnp.bfloat16)
```

```python
import functools

import jax
import jax.numpy as jnp
from jax import lax
from jax.experimental import pallas as pl
from jax.experimental.pallas import tpu as pltpu
from jax.sharding import PartitionSpec as P

MODEL_WIDTH = 8192
QUERY_HEADS = 64
KEYVALUE_HEADS = 8
HEAD_WIDTH = 128
SEGS = 3


EPSILON = 1e-05
ROPE_BASE = 500000.0
MASK_VALUE = -1e30


def row_positions(segments, segment_total):
    bounds = jnp.arange(segment_total + 1, dtype=jnp.int32)
    first_rows = jnp.sum((segments[:, None, :] < bounds[None, :, None]).astype(jnp.int32), axis=2)
    matches = segments[:, :, None] == bounds[None, None, :segment_total]
    segment_first = jnp.sum(jnp.where(matches, first_rows[:, None, :segment_total], 0), axis=2)
    context_length = first_rows[:, 1:2]
    row_index = jnp.arange(segments.shape[1], dtype=jnp.int32)[None, :]
    positions = jnp.where(segments == 0, row_index, context_length + row_index - segment_first)
    return positions.reshape(-1)


def rotate(values, positions):
    half_size = values.shape[-1] // 2
    frequency = ROPE_BASE ** (-2.0 * jnp.arange(half_size, dtype=jnp.float32) / values.shape[-1])
    angle = positions.astype(jnp.float32)[:, None, None] * frequency[None, None, :]
    cosine = jnp.cos(angle)
    sine = jnp.sin(angle)
    first_half = values[..., :half_size]
    second_half = values[..., half_size:]
    return jnp.concatenate(
        [first_half * cosine - second_half * sine, second_half * cosine + first_half * sine],
        axis=-1,
    )


def request_mask(segments):
    row_index = jnp.arange(segments.shape[0], dtype=jnp.int32)
    causal = row_index[None, :] <= row_index[:, None]
    same_part = (segments[None, :] == segments[:, None]) | (segments[None, :] == 0)
    return causal & same_part


def on_device(tokens, norm_gain, w_query, keyvalue_weight, w_out, segment_ids):
    column_group_count = lax.axis_size("gy")
    gy_index = lax.axis_index("gy")
    rows_here = tokens.shape[0]
    query_cols = w_query.shape[1]
    head_block = QUERY_HEADS // column_group_count
    keyvalue_block = KEYVALUE_HEADS // column_group_count
    group_width = QUERY_HEADS // KEYVALUE_HEADS
    query_width = head_block * HEAD_WIDTH
    keyval_width = keyvalue_block * 2 * HEAD_WIDTH
    local_positions = row_positions(segment_ids, SEGS)
    widened = tokens.astype(jnp.float32)
    squares = lax.psum(jnp.sum(widened * widened, axis=1), "gy")
    widened = tokens.astype(jnp.float32)
    normalized_input = (
        widened * lax.rsqrt(squares / MODEL_WIDTH + EPSILON)[:, None] * norm_gain[None, :]
    ).astype(jnp.bfloat16)
    piece_rows = lax.all_gather(normalized_input, "gx", axis=0, tiled=True)
    partial_heads = jnp.concatenate(
        [
            jnp.dot(piece_rows, w_query, preferred_element_type=jnp.float32),
            jnp.dot(piece_rows, keyvalue_weight, preferred_element_type=jnp.float32),
        ],
        axis=1,
    )
    query_part = partial_heads[:, :query_cols]
    keyval_part = partial_heads[:, query_cols:]
    query_sum, keyval_sum = lax.psum((query_part, keyval_part), "gy")
    query_rows, keyval_rows = (
        lax.all_to_all(query_sum, "gx", split_axis=0, concat_axis=1, tiled=True),
        lax.all_to_all(keyval_sum, "gx", split_axis=0, concat_axis=1, tiled=True),
    )
    query_here = lax.dynamic_slice_in_dim(query_rows, gy_index * query_width, query_width, 1)
    keyval_here = lax.dynamic_slice_in_dim(keyval_rows, gy_index * keyval_width, keyval_width, 1)
    heads_of_query = rotate(
        query_here.reshape(rows_here, head_block, HEAD_WIDTH), local_positions
    ).astype(jnp.bfloat16)
    heads_of_query = heads_of_query.reshape(rows_here, keyvalue_block, group_width, HEAD_WIDTH)
    keyvalue_pairs = keyval_here.reshape(rows_here, keyvalue_block, 2, HEAD_WIDTH)
    key_heads = rotate(keyvalue_pairs[:, :, 0], local_positions).astype(jnp.bfloat16)
    value_heads = keyvalue_pairs[:, :, 1].astype(jnp.bfloat16)
    score_scale = HEAD_WIDTH ** (-0.5)
    scores = (
        jnp.einsum("rkgd,tkd->kgrt", heads_of_query, key_heads, preferred_element_type=jnp.float32)
        * score_scale
    )
    visible = request_mask(segment_ids[0])
    scores = jnp.where(visible[None, None], scores, MASK_VALUE)
    row_top = jnp.max(scores, axis=-1, keepdims=True)
    weights = jnp.exp(scores - row_top)
    probabilities = (weights / jnp.sum(weights, axis=-1, keepdims=True)).astype(jnp.bfloat16)
    mixed_heads = jnp.einsum(
        "kgrt,tkd->rkgd", probabilities, value_heads, preferred_element_type=jnp.float32
    )
    mixed = mixed_heads.astype(jnp.bfloat16).reshape(rows_here, query_width)
    output_terms = jnp.dot(
        lax.all_gather(mixed, "gx", axis=0, tiled=True), w_out, preferred_element_type=jnp.float32
    )
    return lax.psum_scatter(output_terms, "gy", scatter_dimension=0, tiled=True).astype(
        jnp.bfloat16
    )


MESH = pl.DeviceIdType.MESH
TILE = 512


def fused_kernel(
    tokens_ref, gain_ref, segments_ref, freq_ref, wq_ref, wkv_ref, wo_ref, out_ref,
    tok_all, stats, normed, wq, wkv, wo, part, recv_a, sum_b, recv_b, final, mixed_send, mixed_all,
    out_acc, out_part, out_recv_a, out_sum_b, out_recv_b,
    local_sem, weight_sem,
    tok_send, tok_recv, stat_send, stat_recv,
    a_send, a_recv, b_send, b_recv, mix_send, mix_recv,
    oa_send, oa_recv, ob_send, ob_recv,
):
    side = 4
    gx = lax.axis_index("gx")
    gy = lax.axis_index("gy")
    chip, core = gy // 2, gy % 2
    me = gx * side + gy
    mate = {"gx": gx, "gy": chip * 2 + (1 - core)}
    across = {"gx": gx, "gy": (1 - chip) * 2 + core}
    rows = tok_all.shape[1]
    width = tok_all.shape[2]
    query_tiles = wq_ref.shape[1] // TILE
    tiles = query_tiles + 1

    own_tokens = pltpu.make_async_copy(tokens_ref, tok_all.at[gx], local_sem.at[0])
    own_tokens.start()
    weight_copies = [pltpu.make_async_copy(wkv_ref, wkv, weight_sem.at[0])]
    for n in range(query_tiles):
        cols = pl.ds(n * TILE, TILE)
        weight_copies.append(
            pltpu.make_async_copy(wq_ref.at[:, cols], wq.at[:, cols], weight_sem.at[1 + n])
        )
    half = wo_ref.shape[0] // 2
    for j in range(2):
        span = pl.ds(j * half, half)
        weight_copies.append(
            pltpu.make_async_copy(wo_ref.at[span, :], wo.at[span, :], weight_sem.at[tiles + j])
        )
    for copy in weight_copies:
        copy.start()

    barrier = pltpu.get_barrier_semaphore()
    for step in range(1, side * side):
        peer = (me + step) % (side * side)
        pl.semaphore_signal(
            barrier, inc=1, device_id={"gx": peer // side, "gy": peer % side}, device_id_type=MESH
        )
    own_tokens.wait()
    mine = tok_all[gx].astype(jnp.float32)
    square_sum = jnp.sum(mine * mine, axis=1, keepdims=True)
    row_id = lax.broadcasted_iota(jnp.int32, (rows, 128), 0)
    col_id = lax.broadcasted_iota(jnp.int32, (rows, 128), 1)
    diagonal = row_id == col_id
    stats[me, 0:1, :] = jnp.sum(jnp.where(diagonal, square_sum, 0.0), axis=0, keepdims=True)
    stats[me, 1:2, :] = segments_ref[...].astype(jnp.float32)
    pl.semaphore_wait(barrier, side * side - 1)

    stat_copies = []
    for step in range(1, side * side):
        peer = (me + step) % (side * side)
        copy = pltpu.make_async_remote_copy(
            src_ref=stats.at[me], dst_ref=stats.at[me],
            send_sem=stat_send.at[step - 1], recv_sem=stat_recv.at[step - 1],
            device_id={"gx": peer // side, "gy": peer % side}, device_id_type=MESH,
        )
        copy.start()
        stat_copies.append(copy)
    tok_copies = []
    for step in range(1, side):
        copy = pltpu.make_async_remote_copy(
            src_ref=tokens_ref, dst_ref=tok_all.at[gx],
            send_sem=tok_send.at[step - 1], recv_sem=tok_recv.at[step - 1],
            device_id={"gx": (gx + step) % side, "gy": gy}, device_id_type=MESH,
        )
        copy.start()
        tok_copies.append(copy)

    for copy in stat_copies:
        copy.wait_recv()

    def as_column(row):
        return jnp.sum(jnp.where(diagonal, row, 0.0), axis=1, keepdims=True)

    segment_row = stats[gy * side + gy, 1:2, :]
    segment_col = as_column(segment_row)
    in_request = col_id < rows
    context = jnp.sum(
        jnp.where(in_request & (segment_row < 0.5), 1.0, 0.0), axis=1, keepdims=True
    )
    first = jnp.sum(
        jnp.where(in_request & (segment_row < segment_col), 1.0, 0.0), axis=1, keepdims=True
    )
    index = row_id[:, 0:1].astype(jnp.float32)
    position = jnp.where(segment_col < 0.5, index, context + index - first)
    angle = position * freq_ref[...]
    cosine = jnp.cos(angle)
    sine = jnp.where(col_id < HEAD_WIDTH // 2, -jnp.sin(angle), jnp.sin(angle))
    visible = (col_id <= row_id) & ((segment_row == segment_col) | (segment_row < 0.5))
    visible = jnp.where(visible, 1.0, 0.0)[:, :rows]
    group_width = QUERY_HEADS // KEYVALUE_HEADS
    visible_all = jnp.concatenate([visible] * group_width, axis=0) > 0.5

    gain = gain_ref[...]
    for step in range(side):
        block = (gx + step) % side if step == 0 else (gx - step + side) % side
        if step > 0:
            tok_copies[step - 1].wait_recv()
        total = stats[block * side, 0:1, :]
        for k in range(1, side):
            total = total + stats[block * side + k, 0:1, :]
        scale = lax.rsqrt(as_column(total) / MODEL_WIDTH + EPSILON)
        normed[block] = (tok_all[block].astype(jnp.float32) * scale * gain).astype(jnp.bfloat16)

    def rotated(values):
        return (values * cosine + pltpu.roll(values, HEAD_WIDTH // 2, 1) * sine).astype(
            jnp.bfloat16
        )

    a_copies, b_copies = [], []

    def project(n):
        weight_copies[n].wait()
        if n == 0:
            weights = wkv[...]
        else:
            weights = wq[:, (n - 1) * TILE : n * TILE]
        value = jnp.dot(
            normed[...].reshape(side * rows, width), weights, preferred_element_type=jnp.float32
        )
        for r in range(side):
            part[n, r % 2, r // 2] = value[r * rows : (r + 1) * rows]
        copy = pltpu.make_async_remote_copy(
            src_ref=part.at[n, 1 - core], dst_ref=recv_a.at[n],
            send_sem=a_send.at[n], recv_sem=a_recv.at[n], device_id=mate, device_id_type=MESH,
        )
        copy.start()
        a_copies.append(copy)

    def pass_on(n):
        a_copies[n].wait_recv()
        sum_b[n] = part[n, core, 1 - chip] + recv_a[n, 1 - chip]
        copy = pltpu.make_async_remote_copy(
            src_ref=sum_b.at[n], dst_ref=recv_b.at[n],
            send_sem=b_send.at[n], recv_sem=b_recv.at[n], device_id=across, device_id_type=MESH,
        )
        copy.start()
        b_copies.append(copy)

    def finish(n):
        b_copies[n].wait_recv()
        return part[n, core, chip] + recv_a[n, chip] + recv_b[n]

    for n in range(tiles):
        project(n)
        if n > 0:
            pass_on(n - 1)
    pass_on(tiles - 1)

    heads_in_tile = TILE // HEAD_WIDTH
    keyval = finish(0)
    local_kv = wkv_ref.shape[1] // (2 * HEAD_WIDTH)
    mix_copies = []
    for j in range(local_kv):
        key_head = rotated(keyval[:, 2 * j * HEAD_WIDTH : (2 * j + 1) * HEAD_WIDTH])
        value_head = keyval[:, (2 * j + 1) * HEAD_WIDTH : (2 * j + 2) * HEAD_WIDTH].astype(
            jnp.bfloat16
        )
        queries = []
        for t in range(group_width // heads_in_tile):
            query_tile = finish(1 + j * (group_width // heads_in_tile) + t)
            for h in range(heads_in_tile):
                queries.append(rotated(query_tile[:, h * HEAD_WIDTH : (h + 1) * HEAD_WIDTH]))
        query = jnp.concatenate(queries, axis=0)
        scores = lax.dot_general(
            query, key_head, (((1,), (1,)), ((), ())), preferred_element_type=jnp.float32
        ) * (HEAD_WIDTH ** (-0.5))
        scores = jnp.where(visible_all, scores, MASK_VALUE)
        weights = jnp.exp(scores - jnp.max(scores, axis=1, keepdims=True))
        probs = (weights / jnp.sum(weights, axis=1, keepdims=True)).astype(jnp.bfloat16)
        mixed = jnp.dot(probs, value_head, preferred_element_type=jnp.float32).astype(jnp.bfloat16)
        for h in range(group_width):
            mixed_send[j, :, h * HEAD_WIDTH : (h + 1) * HEAD_WIDTH] = mixed[
                h * rows : (h + 1) * rows
            ]

        @pl.when(gx == gy)
        def _():
            mixed_all[j, gy] = mixed_send[j]

        for step in (3, 2, 1, 0):
            copy = pltpu.make_async_remote_copy(
                src_ref=mixed_send.at[j], dst_ref=mixed_all.at[j, gy],
                send_sem=mix_send.at[j, step], recv_sem=mix_recv.at[j, gy],
                device_id={"gx": (gx + step) % side, "gy": gx}, device_id_type=MESH,
            )
            if step == 0:
                pl.when(gx != gy)(copy.start)
            else:
                copy.start()
            mix_copies.append((step, copy))

    def wait_mixed(j):
        for step in range(side):
            r = (gy + step) % side
            copy = pltpu.make_async_remote_copy(
                src_ref=mixed_send.at[j], dst_ref=mixed_all.at[j, r],
                send_sem=mix_send.at[j, 0], recv_sem=mix_recv.at[j, r],
                device_id=mate, device_id_type=MESH,
            )
            if step == 0:
                pl.when(gx != gy)(copy.wait_recv)
            else:
                copy.wait_recv()

    out_tiles = wo_ref.shape[1] // TILE
    wait_mixed(0)
    weight_copies[tiles].wait()
    for n in range(out_tiles):
        out_acc[n] = jnp.dot(
            mixed_all[0].reshape(side * rows, half), wo[0:half, n * TILE : (n + 1) * TILE],
            preferred_element_type=jnp.float32,
        )
    wait_mixed(1)
    weight_copies[tiles + 1].wait()

    oa_copies, ob_copies = [], []

    def out_project(n):
        value = out_acc[n] + jnp.dot(
            mixed_all[1].reshape(side * rows, half), wo[half:, n * TILE : (n + 1) * TILE],
            preferred_element_type=jnp.float32,
        )
        for r in range(side):
            out_part[n, r % 2, r // 2] = value[r * rows : (r + 1) * rows]
        copy = pltpu.make_async_remote_copy(
            src_ref=out_part.at[n, 1 - core], dst_ref=out_recv_a.at[n],
            send_sem=oa_send.at[n], recv_sem=oa_recv.at[n], device_id=mate, device_id_type=MESH,
        )
        copy.start()
        oa_copies.append(copy)

    def out_pass_on(n):
        oa_copies[n].wait_recv()
        out_sum_b[n] = out_part[n, core, 1 - chip] + out_recv_a[n, 1 - chip]
        copy = pltpu.make_async_remote_copy(
            src_ref=out_sum_b.at[n], dst_ref=out_recv_b.at[n],
            send_sem=ob_send.at[n], recv_sem=ob_recv.at[n], device_id=across, device_id_type=MESH,
        )
        copy.start()
        ob_copies.append(copy)

    for n in range(out_tiles):
        out_project(n)
        if n > 0:
            out_pass_on(n - 1)
    out_pass_on(out_tiles - 1)
    for n in range(out_tiles):
        ob_copies[n].wait_recv()
        out_ref[:, n * TILE : (n + 1) * TILE] = (
            out_part[n, core, chip] + out_recv_a[n, chip] + out_recv_b[n]
        ).astype(jnp.bfloat16)

    for copy in stat_copies + tok_copies + a_copies + b_copies + oa_copies + ob_copies:
        copy.wait_send()
    for step, copy in mix_copies:
        if step == 0:
            pl.when(gx != gy)(copy.wait_send)
        else:
            copy.wait_send()


def fused_on_device(tokens, norm_gain, w_query, keyvalue_weight, w_out, segment_ids):
    rows, width = tokens.shape
    side = lax.axis_size("gx")
    frequency = ROPE_BASE ** (
        -2.0 * jnp.arange(HEAD_WIDTH // 2, dtype=jnp.float32) / HEAD_WIDTH
    )
    frequency = jnp.concatenate([frequency, frequency])[None, :]
    segments = jnp.pad(segment_ids, ((0, 0), (0, 128 - segment_ids.shape[1])))
    query_tiles = w_query.shape[1] // TILE
    tiles = query_tiles + 1
    out_tiles = w_out.shape[1] // TILE
    half = w_out.shape[0] // 2
    f32, bf16 = jnp.float32, jnp.bfloat16
    dma = pltpu.SemaphoreType.DMA
    vmem = pl.BlockSpec(memory_space=pltpu.VMEM)
    hbm = pl.BlockSpec(memory_space=pl.ANY)
    return pl.pallas_call(
        fused_kernel,
        out_shape=jax.ShapeDtypeStruct((rows, w_out.shape[1]), bf16),
        in_specs=[hbm, vmem, vmem, vmem, hbm, hbm, hbm],
        out_specs=vmem,
        scratch_shapes=[
            pltpu.VMEM((side, rows, width), bf16),
            pltpu.VMEM((side * side, 8, 128), f32),
            pltpu.VMEM((side, rows, width), bf16),
            pltpu.VMEM(w_query.shape, bf16),
            pltpu.VMEM(keyvalue_weight.shape, bf16),
            pltpu.VMEM(w_out.shape, bf16),
            pltpu.VMEM((tiles, 2, 2, rows, TILE), f32),
            pltpu.VMEM((tiles, 2, rows, TILE), f32),
            pltpu.VMEM((tiles, rows, TILE), f32),
            pltpu.VMEM((tiles, rows, TILE), f32),
            pltpu.VMEM((tiles, rows, TILE), f32),
            pltpu.VMEM((2, rows, half), bf16),
            pltpu.VMEM((2, side, rows, half), bf16),
            pltpu.VMEM((out_tiles, side * rows, TILE), f32),
            pltpu.VMEM((out_tiles, 2, 2, rows, TILE), f32),
            pltpu.VMEM((out_tiles, 2, rows, TILE), f32),
            pltpu.VMEM((out_tiles, rows, TILE), f32),
            pltpu.VMEM((out_tiles, rows, TILE), f32),
            dma((1,)), dma((tiles + 2,)),
            dma((side - 1,)), dma((side - 1,)),
            dma((side * side - 1,)), dma((side * side - 1,)),
            dma((tiles,)), dma((tiles,)), dma((tiles,)), dma((tiles,)),
            dma((2, side)), dma((2, side)),
            dma((out_tiles,)), dma((out_tiles,)), dma((out_tiles,)), dma((out_tiles,)),
        ],
        compiler_params=pltpu.CompilerParams(
            collective_id=0, has_side_effects=True, vmem_limit_bytes=48 * 1024 * 1024
        ),
        cost_estimate=pl.CostEstimate(
            flops=2 * side * rows * width * (w_query.shape[1] * 2 + keyvalue_weight.shape[1]),
            bytes_accessed=2 * (w_query.size + keyvalue_weight.size + w_out.size),
            transcendentals=0,
        ),
    )(tokens, norm_gain[None, :], segments, frequency, w_query, keyvalue_weight, w_out)


def program_for(mesh):
    if mesh.shape["gx"] == 4 and mesh.shape["gy"] == 4:
        return fused_on_device
    return on_device


def solution(mesh):
    return jax.shard_map(
        program_for(mesh),
        mesh=mesh,
        in_specs=(
            P(("groups", "gx"), "gy"),
            P("gy"),
            P("gy", "gx"),
            P("gy", "gx"),
            P("gy", "gx"),
            P(("groups", "gx"), None),
        ),
        out_specs=P(("groups", "gy"), "gx"),
        check_vma=False,
    )
```

```python
import math

import jax
import jax.numpy as jnp
from jax import lax
from jax.experimental import pallas as pl
from jax.experimental.pallas import tpu as pltpu
from jax.sharding import PartitionSpec as P

MODEL_WIDTH = 8192
QUERY_HEADS = 64
KEYVALUE_HEADS = 8
HEAD_WIDTH = 128
SEGS = 3


EPSILON = 1e-05
ROPE_BASE = 500000.0
MASK_VALUE = -1e30


def row_positions(segments, segment_total):
    bounds = jnp.arange(segment_total + 1, dtype=jnp.int32)
    first_rows = jnp.sum((segments[:, None, :] < bounds[None, :, None]).astype(jnp.int32), axis=2)
    matches = segments[:, :, None] == bounds[None, None, :segment_total]
    segment_first = jnp.sum(jnp.where(matches, first_rows[:, None, :segment_total], 0), axis=2)
    context_length = first_rows[:, 1:2]
    row_index = jnp.arange(segments.shape[1], dtype=jnp.int32)[None, :]
    positions = jnp.where(segments == 0, row_index, context_length + row_index - segment_first)
    return positions.reshape(-1)


def rotate(values, positions):
    half_size = values.shape[-1] // 2
    frequency = ROPE_BASE ** (-2.0 * jnp.arange(half_size, dtype=jnp.float32) / values.shape[-1])
    angle = positions.astype(jnp.float32)[:, None, None] * frequency[None, None, :]
    cosine = jnp.cos(angle)
    sine = jnp.sin(angle)
    first_half = values[..., :half_size]
    second_half = values[..., half_size:]
    return jnp.concatenate(
        [first_half * cosine - second_half * sine, second_half * cosine + first_half * sine],
        axis=-1,
    )


def request_mask(segments):
    row_index = jnp.arange(segments.shape[0], dtype=jnp.int32)
    causal = row_index[None, :] <= row_index[:, None]
    same_part = (segments[None, :] == segments[:, None]) | (segments[None, :] == 0)
    return causal & same_part


def on_device(tokens, norm_gain, w_query, keyvalue_weight, w_out, segment_ids):
    column_group_count = lax.axis_size("gy")
    gy_index = lax.axis_index("gy")
    rows_here = tokens.shape[0]
    query_cols = w_query.shape[1]
    head_block = QUERY_HEADS // column_group_count
    keyvalue_block = KEYVALUE_HEADS // column_group_count
    group_width = QUERY_HEADS // KEYVALUE_HEADS
    query_width = head_block * HEAD_WIDTH
    keyval_width = keyvalue_block * 2 * HEAD_WIDTH
    local_positions = row_positions(segment_ids, SEGS)
    widened = tokens.astype(jnp.float32)
    squares = lax.psum(jnp.sum(widened * widened, axis=1), "gy")
    widened = tokens.astype(jnp.float32)
    normalized_input = (
        widened * lax.rsqrt(squares / MODEL_WIDTH + EPSILON)[:, None] * norm_gain[None, :]
    ).astype(jnp.bfloat16)
    piece_rows = lax.all_gather(normalized_input, "gx", axis=0, tiled=True)
    partial_heads = jnp.concatenate(
        [
            jnp.dot(piece_rows, w_query, preferred_element_type=jnp.float32),
            jnp.dot(piece_rows, keyvalue_weight, preferred_element_type=jnp.float32),
        ],
        axis=1,
    )
    query_part = partial_heads[:, :query_cols]
    keyval_part = partial_heads[:, query_cols:]
    query_sum, keyval_sum = lax.psum((query_part, keyval_part), "gy")
    query_rows, keyval_rows = (
        lax.all_to_all(query_sum, "gx", split_axis=0, concat_axis=1, tiled=True),
        lax.all_to_all(keyval_sum, "gx", split_axis=0, concat_axis=1, tiled=True),
    )
    query_here = lax.dynamic_slice_in_dim(query_rows, gy_index * query_width, query_width, 1)
    keyval_here = lax.dynamic_slice_in_dim(keyval_rows, gy_index * keyval_width, keyval_width, 1)
    heads_of_query = rotate(
        query_here.reshape(rows_here, head_block, HEAD_WIDTH), local_positions
    ).astype(jnp.bfloat16)
    heads_of_query = heads_of_query.reshape(rows_here, keyvalue_block, group_width, HEAD_WIDTH)
    keyvalue_pairs = keyval_here.reshape(rows_here, keyvalue_block, 2, HEAD_WIDTH)
    key_heads = rotate(keyvalue_pairs[:, :, 0], local_positions).astype(jnp.bfloat16)
    value_heads = keyvalue_pairs[:, :, 1].astype(jnp.bfloat16)
    score_scale = HEAD_WIDTH ** (-0.5)
    scores = (
        jnp.einsum("rkgd,tkd->kgrt", heads_of_query, key_heads, preferred_element_type=jnp.float32)
        * score_scale
    )
    visible = request_mask(segment_ids[0])
    scores = jnp.where(visible[None, None], scores, MASK_VALUE)
    row_top = jnp.max(scores, axis=-1, keepdims=True)
    weights = jnp.exp(scores - row_top)
    probabilities = (weights / jnp.sum(weights, axis=-1, keepdims=True)).astype(jnp.bfloat16)
    mixed_heads = jnp.einsum(
        "kgrt,tkd->rkgd", probabilities, value_heads, preferred_element_type=jnp.float32
    )
    mixed = mixed_heads.astype(jnp.bfloat16).reshape(rows_here, query_width)
    output_terms = jnp.dot(
        lax.all_gather(mixed, "gx", axis=0, tiled=True), w_out, preferred_element_type=jnp.float32
    )
    return lax.psum_scatter(output_terms, "gy", scatter_dimension=0, tiled=True).astype(
        jnp.bfloat16
    )


MESH = pl.DeviceIdType.MESH
TILE = 512
CHUNKS = 4


def fused_kernel(
    tokens_ref, gain_hbm, segments_hbm, wq_ref, wkv_ref, wo_ref, out_ref,
    gain_ref, segments_ref, tok_all, stats, normed, wq, wkv, wo, part, recv_a, sum_b, recv_b, final, mixed_send, mixed_all,
    out_acc, out_part, out_recv_a, out_sum_b, out_recv_b,
    local_sem, weight_sem,
    tok_send, tok_recv, stat_send, stat_recv,
    a_send, a_recv, b_send, b_recv, mix_send, mix_recv,
    oa_send, oa_recv, ob_send, ob_recv,
):
    side = 4
    gx = lax.axis_index("gx")
    gy = lax.axis_index("gy")
    chip, core = gy // 2, gy % 2
    me = gx * side + gy
    mate = {"gx": gx, "gy": chip * 2 + (1 - core)}
    across = {"gx": gx, "gy": (1 - chip) * 2 + core}
    rows = tok_all.shape[2]
    span = tok_all.shape[3]
    query_tiles = wq_ref.shape[1] // TILE
    tiles = query_tiles + 1

    own_tokens = [
        pltpu.make_async_copy(
            tokens_ref.at[:, pl.ds(c * span, span)], tok_all.at[c, gx], local_sem.at[2 + c]
        )
        for c in range(CHUNKS)
    ]
    for copy in own_tokens:
        copy.start()
    own_segments = pltpu.make_async_copy(segments_hbm, segments_ref, local_sem.at[0])
    own_segments.start()
    own_gain = pltpu.make_async_copy(gain_hbm, gain_ref, local_sem.at[1])
    own_gain.start()
    weight_copies = []
    for c in range(CHUNKS):
        piece = pl.ds(c * span, span)
        weight_copies.append(
            pltpu.make_async_copy(wkv_ref.at[piece, :], wkv.at[piece, :], weight_sem.at[2 * c])
        )
        weight_copies.append(
            pltpu.make_async_copy(wq_ref.at[piece, :], wq.at[piece, :], weight_sem.at[2 * c + 1])
        )
    half = wo_ref.shape[0] // 2
    for j in range(2):
        piece = pl.ds(j * half, half)
        weight_copies.append(
            pltpu.make_async_copy(wo_ref.at[piece, :], wo.at[piece, :], weight_sem.at[2 * CHUNKS + j])
        )
    for copy in weight_copies[: 2 * CHUNKS]:
        copy.start()

    barrier = pltpu.get_barrier_semaphore()
    for step in range(1, side * side):
        peer = (me + step) % (side * side)
        pl.semaphore_signal(
            barrier, inc=1, device_id={"gx": peer // side, "gy": peer % side}, device_id_type=MESH
        )
    square_sum = jnp.zeros((rows, 1), jnp.float32)
    for c in range(CHUNKS):
        own_tokens[c].wait()
        mine = tok_all[c, gx].astype(jnp.float32)
        square_sum += jnp.sum(mine * mine, axis=1, keepdims=True)
    row_id = lax.broadcasted_iota(jnp.int32, (rows, 128), 0)
    col_id = lax.broadcasted_iota(jnp.int32, (rows, 128), 1)
    diagonal = row_id == col_id
    stats[me] = jnp.zeros(stats.shape[1:], jnp.float32)
    stats[me, 0:1, :] = jnp.sum(jnp.where(diagonal, square_sum, 0.0), axis=0, keepdims=True)
    own_segments.wait()
    stats[me, 1:2, 0:rows] = segments_ref[...].astype(jnp.float32)
    half_index = (col_id % (HEAD_WIDTH // 2)).astype(jnp.float32)
    table_angle = row_id.astype(jnp.float32) * jnp.exp(
        half_index * (-2.0 * math.log(ROPE_BASE) / HEAD_WIDTH)
    )
    cosine_table = jnp.cos(table_angle)
    sine_table = jnp.sin(table_angle)
    sine_table = jnp.where(col_id < HEAD_WIDTH // 2, -sine_table, sine_table)
    pl.semaphore_wait(barrier, side * side - 1)

    stat_copies = []
    for step in range(1, side * side):
        peer = (me + step) % (side * side)
        copy = pltpu.make_async_remote_copy(
            src_ref=stats.at[me], dst_ref=stats.at[me],
            send_sem=stat_send.at[step - 1], recv_sem=stat_recv.at[step - 1],
            device_id={"gx": peer // side, "gy": peer % side}, device_id_type=MESH,
        )
        copy.start()
        stat_copies.append(copy)
    middle = (gx == 1) | (gx == 2)
    outer = 3 * (gx // 2)
    far = 3 - outer

    def token_copy(c, slot, block, target):
        return pltpu.make_async_remote_copy(
            src_ref=tok_all.at[c, block], dst_ref=tok_all.at[c, block],
            send_sem=tok_send.at[c, slot], recv_sem=tok_recv.at[c, block],
            device_id={"gx": target, "gy": gy}, device_id_type=MESH,
        )

    for c in range(CHUNKS):
        token_copy(c, 1, gx, (gx + 2) % side).start()
        token_copy(c, 0, gx, 1 + gx % 2).start()
        pl.when(middle)(token_copy(c, 2, gx, outer).start)
    for copy in weight_copies[2 * CHUNKS :]:
        copy.start()

    def hand_on(c):
        @pl.when(middle)
        def _():
            copy = token_copy(c, 3, far, outer)
            copy.wait_recv()
            copy.start()

    for copy in stat_copies:
        copy.wait_recv()

    def as_column(row):
        return jnp.sum(jnp.where(diagonal, row, 0.0), axis=1, keepdims=True)

    segment_row = stats[gy * side + gy, 1:2, :]
    segment_col = as_column(segment_row)
    in_request = col_id < rows
    context = jnp.sum(
        jnp.where(in_request & (segment_row < 0.5), 1.0, 0.0), axis=1, keepdims=True
    )
    first = jnp.sum(
        jnp.where(in_request & (segment_row < segment_col), 1.0, 0.0), axis=1, keepdims=True
    )
    index = row_id[:, 0:1].astype(jnp.float32)
    position = jnp.where(segment_col < 0.5, index, context + index - first)
    cosine = jnp.zeros((rows, HEAD_WIDTH), jnp.float32)
    sine = jnp.zeros((rows, HEAD_WIDTH), jnp.float32)
    for p in range(rows):
        here = position == float(p)
        cosine = jnp.where(here, cosine_table[p : p + 1], cosine)
        sine = jnp.where(here, sine_table[p : p + 1], sine)
    visible = (col_id <= row_id) & ((segment_row == segment_col) | (segment_row < 0.5))
    visible = jnp.where(visible, 1.0, 0.0)[:, :rows]
    group_width = QUERY_HEADS // KEYVALUE_HEADS
    visible_all = jnp.concatenate([visible] * group_width, axis=0) > 0.5

    own_gain.wait()
    scales = []
    for block in range(side):
        total = stats[block * side, 0:1, :]
        for k in range(1, side):
            total = total + stats[block * side + k, 0:1, :]
        scales.append(lax.rsqrt(as_column(total) / MODEL_WIDTH + EPSILON))

    def rotated(values):
        return (values * cosine + pltpu.roll(values, HEAD_WIDTH // 2, 1) * sine).astype(
            jnp.bfloat16
        )

    a_copies, b_copies = [], []

    def normalize(c):
        for step in (1, 3, 2):
            copy = token_copy(c, 0, (gx + step) % side, outer)
            if step == 2:
                pl.when(jnp.logical_not(middle))(copy.wait_recv)
            else:
                copy.wait_recv()
        gain = gain_ref[:, c * span : (c + 1) * span]
        for block in range(side):
            normed[c, block] = (
                tok_all[c, block].astype(jnp.float32) * scales[block] * gain
            ).astype(jnp.bfloat16)
        weight_copies[2 * c].wait()
        weight_copies[2 * c + 1].wait()

    def project(c, n):
        piece = slice(c * span, (c + 1) * span)
        weights = wkv[piece, :] if n == 0 else wq[piece, (n - 1) * TILE : n * TILE]
        value = jnp.dot(
            normed[c].reshape(side * rows, span), weights, preferred_element_type=jnp.float32
        )
        for r in range(side):
            term = value[r * rows : (r + 1) * rows]
            part[n, r % 2, r // 2] = term if c == 0 else part[n, r % 2, r // 2] + term

    def give_mate(n):
        copy = pltpu.make_async_remote_copy(
            src_ref=part.at[n, 1 - core], dst_ref=recv_a.at[n],
            send_sem=a_send.at[n], recv_sem=a_recv.at[n], device_id=mate, device_id_type=MESH,
        )
        copy.start()
        a_copies.append(copy)

    def pass_on(n):
        a_copies[n].wait_recv()
        sum_b[n] = part[n, core, 1 - chip] + recv_a[n, 1 - chip]
        copy = pltpu.make_async_remote_copy(
            src_ref=sum_b.at[n], dst_ref=recv_b.at[n],
            send_sem=b_send.at[n], recv_sem=b_recv.at[n], device_id=across, device_id_type=MESH,
        )
        copy.start()
        b_copies.append(copy)

    def finish(n):
        b_copies[n].wait_recv()
        return part[n, core, chip] + recv_a[n, chip] + recv_b[n]

    hand_on(0)
    for c in range(CHUNKS - 1):
        hand_on(c + 1)
        normalize(c)
        for n in range(tiles):
            project(c, n)
    normalize(CHUNKS - 1)
    for n in range(tiles):
        project(CHUNKS - 1, n)
        give_mate(n)
        if n > 0:
            pass_on(n - 1)
    pass_on(tiles - 1)

    heads_in_tile = TILE // HEAD_WIDTH
    keyval = finish(0)
    local_kv = wkv_ref.shape[1] // (2 * HEAD_WIDTH)
    mix_copies = []
    for j in range(local_kv):
        key_head = rotated(keyval[:, 2 * j * HEAD_WIDTH : (2 * j + 1) * HEAD_WIDTH])
        value_head = keyval[:, (2 * j + 1) * HEAD_WIDTH : (2 * j + 2) * HEAD_WIDTH].astype(
            jnp.bfloat16
        )
        queries = []
        for t in range(group_width // heads_in_tile):
            query_tile = finish(1 + j * (group_width // heads_in_tile) + t)
            for h in range(heads_in_tile):
                queries.append(rotated(query_tile[:, h * HEAD_WIDTH : (h + 1) * HEAD_WIDTH]))
        query = jnp.concatenate(queries, axis=0)
        scores = lax.dot_general(
            query, key_head, (((1,), (1,)), ((), ())), preferred_element_type=jnp.float32
        ) * (HEAD_WIDTH ** (-0.5))
        scores = jnp.where(visible_all, scores, MASK_VALUE)
        weights = jnp.exp(scores - jnp.max(scores, axis=1, keepdims=True))
        probs = (weights / jnp.sum(weights, axis=1, keepdims=True)).astype(jnp.bfloat16)
        mixed = jnp.dot(probs, value_head, preferred_element_type=jnp.float32).astype(jnp.bfloat16)
        for h in range(group_width):
            mixed_send[j, :, h * HEAD_WIDTH : (h + 1) * HEAD_WIDTH] = mixed[
                h * rows : (h + 1) * rows
            ]

        @pl.when(gx == gy)
        def _():
            mixed_all[j, gy] = mixed_send[j]

        for step in (3, 2, 1, 0):
            copy = pltpu.make_async_remote_copy(
                src_ref=mixed_send.at[j], dst_ref=mixed_all.at[j, gy],
                send_sem=mix_send.at[j, step], recv_sem=mix_recv.at[j, gy],
                device_id={"gx": (gx + step) % side, "gy": gx}, device_id_type=MESH,
            )
            if step == 0:
                pl.when(gx != gy)(copy.start)
            else:
                copy.start()
            mix_copies.append((step, copy))

    def wait_mixed(j):
        for step in range(side):
            r = (gy + step) % side
            copy = pltpu.make_async_remote_copy(
                src_ref=mixed_send.at[j], dst_ref=mixed_all.at[j, r],
                send_sem=mix_send.at[j, 0], recv_sem=mix_recv.at[j, r],
                device_id=mate, device_id_type=MESH,
            )
            if step == 0:
                pl.when(gx != gy)(copy.wait_recv)
            else:
                copy.wait_recv()

    out_tiles = wo_ref.shape[1] // TILE
    wait_mixed(0)
    weight_copies[2 * CHUNKS].wait()
    for n in range(out_tiles):
        out_acc[n] = jnp.dot(
            mixed_all[0].reshape(side * rows, half), wo[0:half, n * TILE : (n + 1) * TILE],
            preferred_element_type=jnp.float32,
        )
    wait_mixed(1)
    weight_copies[2 * CHUNKS + 1].wait()

    oa_copies, ob_copies = [], []

    def out_project(n):
        value = out_acc[n] + jnp.dot(
            mixed_all[1].reshape(side * rows, half), wo[half:, n * TILE : (n + 1) * TILE],
            preferred_element_type=jnp.float32,
        )
        for r in range(side):
            out_part[n, r % 2, r // 2] = value[r * rows : (r + 1) * rows]
        copy = pltpu.make_async_remote_copy(
            src_ref=out_part.at[n, 1 - core], dst_ref=out_recv_a.at[n],
            send_sem=oa_send.at[n], recv_sem=oa_recv.at[n], device_id=mate, device_id_type=MESH,
        )
        copy.start()
        oa_copies.append(copy)

    def out_pass_on(n):
        oa_copies[n].wait_recv()
        out_sum_b[n] = out_part[n, core, 1 - chip] + out_recv_a[n, 1 - chip]
        copy = pltpu.make_async_remote_copy(
            src_ref=out_sum_b.at[n], dst_ref=out_recv_b.at[n],
            send_sem=ob_send.at[n], recv_sem=ob_recv.at[n], device_id=across, device_id_type=MESH,
        )
        copy.start()
        ob_copies.append(copy)

    for n in range(out_tiles):
        out_project(n)
        if n > 0:
            out_pass_on(n - 1)
    out_pass_on(out_tiles - 1)
    for n in range(out_tiles):
        ob_copies[n].wait_recv()
        out_ref[:, n * TILE : (n + 1) * TILE] = (
            out_part[n, core, chip] + out_recv_a[n, chip] + out_recv_b[n]
        ).astype(jnp.bfloat16)

    for c in range(CHUNKS):
        token_copy(c, 0, gx, outer).wait_send()
        token_copy(c, 1, gx, outer).wait_send()

        @pl.when(middle)
        def _():
            token_copy(c, 2, gx, outer).wait_send()
            token_copy(c, 3, far, outer).wait_send()

    for copy in stat_copies + a_copies + b_copies + oa_copies + ob_copies:
        copy.wait_send()
    for step, copy in mix_copies:
        if step == 0:
            pl.when(gx != gy)(copy.wait_send)
        else:
            copy.wait_send()


def fused_on_device(tokens, norm_gain, w_query, keyvalue_weight, w_out, segment_ids):
    rows, width = tokens.shape
    side = lax.axis_size("gx")
    query_tiles = w_query.shape[1] // TILE
    tiles = query_tiles + 1
    out_tiles = w_out.shape[1] // TILE
    half = w_out.shape[0] // 2
    f32, bf16 = jnp.float32, jnp.bfloat16
    dma = pltpu.SemaphoreType.DMA
    vmem = pl.BlockSpec(memory_space=pltpu.VMEM)
    hbm = pl.BlockSpec(memory_space=pl.ANY)
    return pl.pallas_call(
        fused_kernel,
        out_shape=jax.ShapeDtypeStruct((rows, w_out.shape[1]), bf16),
        in_specs=[hbm] * 6,
        out_specs=vmem,
        scratch_shapes=[
            pltpu.VMEM((1, width), f32),
            pltpu.VMEM(segment_ids.shape, jnp.int32),
            pltpu.VMEM((CHUNKS, side, rows, width // CHUNKS), bf16),
            pltpu.VMEM((side * side, 8, 128), f32),
            pltpu.VMEM((CHUNKS, side, rows, width // CHUNKS), bf16),
            pltpu.VMEM(w_query.shape, bf16),
            pltpu.VMEM(keyvalue_weight.shape, bf16),
            pltpu.VMEM(w_out.shape, bf16),
            pltpu.VMEM((tiles, 2, 2, rows, TILE), f32),
            pltpu.VMEM((tiles, 2, rows, TILE), f32),
            pltpu.VMEM((tiles, rows, TILE), f32),
            pltpu.VMEM((tiles, rows, TILE), f32),
            pltpu.VMEM((tiles, rows, TILE), f32),
            pltpu.VMEM((2, rows, half), bf16),
            pltpu.VMEM((2, side, rows, half), bf16),
            pltpu.VMEM((out_tiles, side * rows, TILE), f32),
            pltpu.VMEM((out_tiles, 2, 2, rows, TILE), f32),
            pltpu.VMEM((out_tiles, 2, rows, TILE), f32),
            pltpu.VMEM((out_tiles, rows, TILE), f32),
            pltpu.VMEM((out_tiles, rows, TILE), f32),
            dma((2 + CHUNKS,)), dma((2 * CHUNKS + 2,)),
            dma((CHUNKS, side)), dma((CHUNKS, side)),
            dma((side * side - 1,)), dma((side * side - 1,)),
            dma((tiles,)), dma((tiles,)), dma((tiles,)), dma((tiles,)),
            dma((2, side)), dma((2, side)),
            dma((out_tiles,)), dma((out_tiles,)), dma((out_tiles,)), dma((out_tiles,)),
        ],
        compiler_params=pltpu.CompilerParams(
            collective_id=0, has_side_effects=True, vmem_limit_bytes=63 * 1024 * 1024
        ),
        cost_estimate=pl.CostEstimate(
            flops=2 * side * rows * width * (w_query.shape[1] * 2 + keyvalue_weight.shape[1]),
            bytes_accessed=2 * (w_query.size + keyvalue_weight.size + w_out.size),
            transcendentals=0,
        ),
    )(tokens, norm_gain[None, :], segment_ids, w_query, keyvalue_weight, w_out)


def program_for(mesh):
    if mesh.shape["gx"] == 4 and mesh.shape["gy"] == 4:
        return fused_on_device
    return on_device


def solution(mesh):
    return jax.shard_map(
        program_for(mesh),
        mesh=mesh,
        in_specs=(
            P(("groups", "gx"), "gy"),
            P("gy"),
            P("gy", "gx"),
            P("gy", "gx"),
            P("gy", "gx"),
            P(("groups", "gx"), None),
        ),
        out_specs=P(("groups", "gy"), "gx"),
        check_vma=False,
    )
```

```python
import math

import jax
import jax.numpy as jnp
from jax import lax
from jax.experimental import pallas as pl
from jax.experimental.pallas import tpu as pltpu
from jax.sharding import PartitionSpec as P

MODEL_WIDTH = 8192
QUERY_HEADS = 64
KEYVALUE_HEADS = 8
HEAD_WIDTH = 128
SEGS = 3


EPSILON = 1e-05
ROPE_BASE = 500000.0
MASK_VALUE = -1e30


def row_positions(segments, segment_total):
    bounds = jnp.arange(segment_total + 1, dtype=jnp.int32)
    first_rows = jnp.sum((segments[:, None, :] < bounds[None, :, None]).astype(jnp.int32), axis=2)
    matches = segments[:, :, None] == bounds[None, None, :segment_total]
    segment_first = jnp.sum(jnp.where(matches, first_rows[:, None, :segment_total], 0), axis=2)
    context_length = first_rows[:, 1:2]
    row_index = jnp.arange(segments.shape[1], dtype=jnp.int32)[None, :]
    positions = jnp.where(segments == 0, row_index, context_length + row_index - segment_first)
    return positions.reshape(-1)


def rotate(values, positions):
    half_size = values.shape[-1] // 2
    frequency = ROPE_BASE ** (-2.0 * jnp.arange(half_size, dtype=jnp.float32) / values.shape[-1])
    angle = positions.astype(jnp.float32)[:, None, None] * frequency[None, None, :]
    cosine = jnp.cos(angle)
    sine = jnp.sin(angle)
    first_half = values[..., :half_size]
    second_half = values[..., half_size:]
    return jnp.concatenate(
        [first_half * cosine - second_half * sine, second_half * cosine + first_half * sine],
        axis=-1,
    )


def request_mask(segments):
    row_index = jnp.arange(segments.shape[0], dtype=jnp.int32)
    causal = row_index[None, :] <= row_index[:, None]
    same_part = (segments[None, :] == segments[:, None]) | (segments[None, :] == 0)
    return causal & same_part


def on_device(tokens, norm_gain, w_query, keyvalue_weight, w_out, segment_ids):
    column_group_count = lax.axis_size("gy")
    gy_index = lax.axis_index("gy")
    rows_here = tokens.shape[0]
    query_cols = w_query.shape[1]
    head_block = QUERY_HEADS // column_group_count
    keyvalue_block = KEYVALUE_HEADS // column_group_count
    group_width = QUERY_HEADS // KEYVALUE_HEADS
    query_width = head_block * HEAD_WIDTH
    keyval_width = keyvalue_block * 2 * HEAD_WIDTH
    local_positions = row_positions(segment_ids, SEGS)
    widened = tokens.astype(jnp.float32)
    squares = lax.psum(jnp.sum(widened * widened, axis=1), "gy")
    widened = tokens.astype(jnp.float32)
    normalized_input = (
        widened * lax.rsqrt(squares / MODEL_WIDTH + EPSILON)[:, None] * norm_gain[None, :]
    ).astype(jnp.bfloat16)
    piece_rows = lax.all_gather(normalized_input, "gx", axis=0, tiled=True)
    partial_heads = jnp.concatenate(
        [
            jnp.dot(piece_rows, w_query, preferred_element_type=jnp.float32),
            jnp.dot(piece_rows, keyvalue_weight, preferred_element_type=jnp.float32),
        ],
        axis=1,
    )
    query_part = partial_heads[:, :query_cols]
    keyval_part = partial_heads[:, query_cols:]
    query_sum, keyval_sum = lax.psum((query_part, keyval_part), "gy")
    query_rows, keyval_rows = (
        lax.all_to_all(query_sum, "gx", split_axis=0, concat_axis=1, tiled=True),
        lax.all_to_all(keyval_sum, "gx", split_axis=0, concat_axis=1, tiled=True),
    )
    query_here = lax.dynamic_slice_in_dim(query_rows, gy_index * query_width, query_width, 1)
    keyval_here = lax.dynamic_slice_in_dim(keyval_rows, gy_index * keyval_width, keyval_width, 1)
    heads_of_query = rotate(
        query_here.reshape(rows_here, head_block, HEAD_WIDTH), local_positions
    ).astype(jnp.bfloat16)
    heads_of_query = heads_of_query.reshape(rows_here, keyvalue_block, group_width, HEAD_WIDTH)
    keyvalue_pairs = keyval_here.reshape(rows_here, keyvalue_block, 2, HEAD_WIDTH)
    key_heads = rotate(keyvalue_pairs[:, :, 0], local_positions).astype(jnp.bfloat16)
    value_heads = keyvalue_pairs[:, :, 1].astype(jnp.bfloat16)
    score_scale = HEAD_WIDTH ** (-0.5)
    scores = (
        jnp.einsum("rkgd,tkd->kgrt", heads_of_query, key_heads, preferred_element_type=jnp.float32)
        * score_scale
    )
    visible = request_mask(segment_ids[0])
    scores = jnp.where(visible[None, None], scores, MASK_VALUE)
    row_top = jnp.max(scores, axis=-1, keepdims=True)
    weights = jnp.exp(scores - row_top)
    probabilities = (weights / jnp.sum(weights, axis=-1, keepdims=True)).astype(jnp.bfloat16)
    mixed_heads = jnp.einsum(
        "kgrt,tkd->rkgd", probabilities, value_heads, preferred_element_type=jnp.float32
    )
    mixed = mixed_heads.astype(jnp.bfloat16).reshape(rows_here, query_width)
    output_terms = jnp.dot(
        lax.all_gather(mixed, "gx", axis=0, tiled=True), w_out, preferred_element_type=jnp.float32
    )
    return lax.psum_scatter(output_terms, "gy", scatter_dimension=0, tiled=True).astype(
        jnp.bfloat16
    )


MESH = pl.DeviceIdType.MESH
TILE = 512
CHUNKS = 2


def fused_kernel(
    tokens_ref, gain_hbm, segments_hbm, wq_ref, wkv_ref, wo_ref, out_ref,
    gain_ref, segments_ref, tok_all, stats, normed, wq, wkv, wo, part, recv_a, sum_b, recv_b, final, mixed_send, mixed_all,
    out_acc, out_part, out_recv_a, out_sum_b, out_recv_b,
    local_sem, weight_sem,
    tok_send, tok_recv, stat_send, stat_recv,
    a_send, a_recv, b_send, b_recv, mix_send, mix_recv,
    oa_send, oa_recv, ob_send, ob_recv,
):
    side = 4
    gx = lax.axis_index("gx")
    gy = lax.axis_index("gy")
    chip, core = gy // 2, gy % 2
    me = gx * side + gy
    mate = {"gx": gx, "gy": chip * 2 + (1 - core)}
    across = {"gx": gx, "gy": (1 - chip) * 2 + core}
    rows = tok_all.shape[2]
    span = tok_all.shape[3]
    query_tiles = wq_ref.shape[1] // TILE
    tiles = query_tiles + 1

    own_tokens = [
        pltpu.make_async_copy(
            tokens_ref.at[:, pl.ds(c * span, span)], tok_all.at[c, gx], local_sem.at[2 + c]
        )
        for c in range(CHUNKS)
    ]
    for copy in own_tokens:
        copy.start()
    own_segments = pltpu.make_async_copy(segments_hbm, segments_ref, local_sem.at[0])
    own_segments.start()
    own_gain = pltpu.make_async_copy(gain_hbm, gain_ref, local_sem.at[1])
    own_gain.start()
    weight_copies = []
    for c in range(CHUNKS):
        piece = pl.ds(c * span, span)
        weight_copies.append(
            pltpu.make_async_copy(wkv_ref.at[piece, :], wkv.at[piece, :], weight_sem.at[2 * c])
        )
        weight_copies.append(
            pltpu.make_async_copy(wq_ref.at[piece, :], wq.at[piece, :], weight_sem.at[2 * c + 1])
        )
    half = wo_ref.shape[0] // 2
    for j in range(2):
        piece = pl.ds(j * half, half)
        weight_copies.append(
            pltpu.make_async_copy(wo_ref.at[piece, :], wo.at[piece, :], weight_sem.at[2 * CHUNKS + j])
        )
    for copy in weight_copies[: 2 * CHUNKS]:
        copy.start()

    barrier = pltpu.get_barrier_semaphore()
    for step in range(1, side * side):
        peer = (me + step) % (side * side)
        pl.semaphore_signal(
            barrier, inc=1, device_id={"gx": peer // side, "gy": peer % side}, device_id_type=MESH
        )
    square_sum = jnp.zeros((rows, 1), jnp.float32)
    for c in range(CHUNKS):
        own_tokens[c].wait()
        mine = tok_all[c, gx].astype(jnp.float32)
        square_sum += jnp.sum(mine * mine, axis=1, keepdims=True)
    row_id = lax.broadcasted_iota(jnp.int32, (rows, 128), 0)
    col_id = lax.broadcasted_iota(jnp.int32, (rows, 128), 1)
    diagonal = row_id == col_id
    stats[me] = jnp.zeros(stats.shape[1:], jnp.float32)
    stats[me, 0:1, :] = jnp.sum(jnp.where(diagonal, square_sum, 0.0), axis=0, keepdims=True)
    own_segments.wait()
    stats[me, 1:2, 0:rows] = segments_ref[...].astype(jnp.float32)
    half_index = (col_id % (HEAD_WIDTH // 2)).astype(jnp.float32)
    table_angle = row_id.astype(jnp.float32) * jnp.exp(
        half_index * (-2.0 * math.log(ROPE_BASE) / HEAD_WIDTH)
    )
    cosine_table = jnp.cos(table_angle)
    sine_table = jnp.sin(table_angle)
    sine_table = jnp.where(col_id < HEAD_WIDTH // 2, -sine_table, sine_table)
    pl.semaphore_wait(barrier, side * side - 1)

    stat_copies = []
    for step in range(1, side * side):
        peer = (me + step) % (side * side)
        copy = pltpu.make_async_remote_copy(
            src_ref=stats.at[me], dst_ref=stats.at[me],
            send_sem=stat_send.at[step - 1], recv_sem=stat_recv.at[step - 1],
            device_id={"gx": peer // side, "gy": peer % side}, device_id_type=MESH,
        )
        copy.start()
        stat_copies.append(copy)
    middle = (gx == 1) | (gx == 2)
    outer = 3 * (gx // 2)
    far = 3 - outer

    def token_copy(c, slot, block, target):
        return pltpu.make_async_remote_copy(
            src_ref=tok_all.at[c, block], dst_ref=tok_all.at[c, block],
            send_sem=tok_send.at[c, slot], recv_sem=tok_recv.at[c, block],
            device_id={"gx": target, "gy": gy}, device_id_type=MESH,
        )

    for c in range(CHUNKS):
        token_copy(c, 1, gx, (gx + 2) % side).start()
        token_copy(c, 0, gx, 1 + gx % 2).start()
        pl.when(middle)(token_copy(c, 2, gx, outer).start)
    for copy in weight_copies[2 * CHUNKS :]:
        copy.start()

    def hand_on(c):
        @pl.when(middle)
        def _():
            copy = token_copy(c, 3, far, outer)
            copy.wait_recv()
            copy.start()

    for copy in stat_copies:
        copy.wait_recv()

    def as_column(row):
        return jnp.sum(jnp.where(diagonal, row, 0.0), axis=1, keepdims=True)

    segment_row = stats[gy * side + gy, 1:2, :]
    segment_col = as_column(segment_row)
    in_request = col_id < rows
    context = jnp.sum(
        jnp.where(in_request & (segment_row < 0.5), 1.0, 0.0), axis=1, keepdims=True
    )
    first = jnp.sum(
        jnp.where(in_request & (segment_row < segment_col), 1.0, 0.0), axis=1, keepdims=True
    )
    index = row_id[:, 0:1].astype(jnp.float32)
    position = jnp.where(segment_col < 0.5, index, context + index - first)
    cosine = jnp.zeros((rows, HEAD_WIDTH), jnp.float32)
    sine = jnp.zeros((rows, HEAD_WIDTH), jnp.float32)
    for p in range(rows):
        here = position == float(p)
        cosine = jnp.where(here, cosine_table[p : p + 1], cosine)
        sine = jnp.where(here, sine_table[p : p + 1], sine)
    visible = (col_id <= row_id) & ((segment_row == segment_col) | (segment_row < 0.5))
    visible = jnp.where(visible, 1.0, 0.0)[:, :rows]
    group_width = QUERY_HEADS // KEYVALUE_HEADS
    visible_all = jnp.concatenate([visible] * (TILE // HEAD_WIDTH), axis=0) > 0.5

    own_gain.wait()
    scales = []
    for block in range(side):
        total = stats[block * side, 0:1, :]
        for k in range(1, side):
            total = total + stats[block * side + k, 0:1, :]
        scales.append(lax.rsqrt(as_column(total) / MODEL_WIDTH + EPSILON))

    def rotated(values):
        return (values * cosine + pltpu.roll(values, HEAD_WIDTH // 2, 1) * sine).astype(
            jnp.bfloat16
        )

    a_copies, b_copies = [], []

    def normalize(c):
        for step in (1, 3, 2):
            copy = token_copy(c, 0, (gx + step) % side, outer)
            if step == 2:
                pl.when(jnp.logical_not(middle))(copy.wait_recv)
            else:
                copy.wait_recv()
        gain = gain_ref[:, c * span : (c + 1) * span]
        for block in range(side):
            normed[c, block] = (
                tok_all[c, block].astype(jnp.float32) * scales[block] * gain
            ).astype(jnp.bfloat16)
        weight_copies[2 * c].wait()
        weight_copies[2 * c + 1].wait()

    def project(c, n):
        piece = slice(c * span, (c + 1) * span)
        weights = wkv[piece, :] if n == 0 else wq[piece, (n - 1) * TILE : n * TILE]
        value = jnp.dot(
            normed[c].reshape(side * rows, span), weights, preferred_element_type=jnp.float32
        )
        for r in range(side):
            term = value[r * rows : (r + 1) * rows]
            part[n, r % 2, r // 2] = term if c == 0 else part[n, r % 2, r // 2] + term

    def give_mate(n):
        copy = pltpu.make_async_remote_copy(
            src_ref=part.at[n, 1 - core], dst_ref=recv_a.at[n],
            send_sem=a_send.at[n], recv_sem=a_recv.at[n], device_id=mate, device_id_type=MESH,
        )
        copy.start()
        a_copies.append(copy)

    def pass_on(n):
        a_copies[n].wait_recv()
        sum_b[n] = part[n, core, 1 - chip] + recv_a[n, 1 - chip]
        copy = pltpu.make_async_remote_copy(
            src_ref=sum_b.at[n], dst_ref=recv_b.at[n],
            send_sem=b_send.at[n], recv_sem=b_recv.at[n], device_id=across, device_id_type=MESH,
        )
        copy.start()
        b_copies.append(copy)

    def finish(n):
        b_copies[n].wait_recv()
        return part[n, core, chip] + recv_a[n, chip] + recv_b[n]

    hand_on(0)
    for c in range(CHUNKS - 1):
        hand_on(c + 1)
        normalize(c)
        for n in range(tiles):
            project(c, n)
    normalize(CHUNKS - 1)
    for n in range(tiles):
        project(CHUNKS - 1, n)
        give_mate(n)
        if n > 2:
            pass_on(n - 3)
    for n in range(tiles - 3, tiles):
        pass_on(n)

    heads_in_tile = TILE // HEAD_WIDTH
    keyval = finish(0)
    mix_copies = []
    key_head = value_head = None
    for t in range(query_tiles):
        if t * heads_in_tile % group_width == 0:
            j = t * heads_in_tile // group_width
            key_head = rotated(keyval[:, 2 * j * HEAD_WIDTH : (2 * j + 1) * HEAD_WIDTH])
            value_head = keyval[:, (2 * j + 1) * HEAD_WIDTH : (2 * j + 2) * HEAD_WIDTH].astype(
                jnp.bfloat16
            )
        query_tile = finish(1 + t)
        query = jnp.concatenate(
            [
                rotated(query_tile[:, h * HEAD_WIDTH : (h + 1) * HEAD_WIDTH])
                for h in range(heads_in_tile)
            ],
            axis=0,
        )
        scores = lax.dot_general(
            query, key_head, (((1,), (1,)), ((), ())), preferred_element_type=jnp.float32
        ) * (HEAD_WIDTH ** (-0.5))
        scores = jnp.where(visible_all, scores, MASK_VALUE)
        weights = jnp.exp(scores - jnp.max(scores, axis=1, keepdims=True))
        probs = (weights / jnp.sum(weights, axis=1, keepdims=True)).astype(jnp.bfloat16)
        mixed = jnp.dot(probs, value_head, preferred_element_type=jnp.float32).astype(jnp.bfloat16)
        for h in range(heads_in_tile):
            mixed_send[t, :, h * HEAD_WIDTH : (h + 1) * HEAD_WIDTH] = mixed[
                h * rows : (h + 1) * rows
            ]

        @pl.when(gx == gy)
        def _():
            mixed_all[t, gy] = mixed_send[t]

        for step in (3, 2, 1, 0):
            copy = pltpu.make_async_remote_copy(
                src_ref=mixed_send.at[t], dst_ref=mixed_all.at[t, gy],
                send_sem=mix_send.at[t, step], recv_sem=mix_recv.at[t, gy],
                device_id={"gx": (gx + step) % side, "gy": gx}, device_id_type=MESH,
            )
            if step == 0:
                pl.when(gx != gy)(copy.start)
            else:
                copy.start()
            mix_copies.append((step, copy))

    def wait_mixed(t):
        for step in range(side):
            r = (gy + step) % side
            copy = pltpu.make_async_remote_copy(
                src_ref=mixed_send.at[t], dst_ref=mixed_all.at[t, r],
                send_sem=mix_send.at[t, 0], recv_sem=mix_recv.at[t, r],
                device_id=mate, device_id_type=MESH,
            )
            if step == 0:
                pl.when(gx != gy)(copy.wait_recv)
            else:
                copy.wait_recv()

    out_tiles = wo_ref.shape[1] // TILE

    def out_term(t, n):
        return jnp.dot(
            mixed_all[t].reshape(side * rows, TILE),
            wo[t * TILE : (t + 1) * TILE, n * TILE : (n + 1) * TILE],
            preferred_element_type=jnp.float32,
        )

    for t in range(query_tiles - 1):
        wait_mixed(t)
        if t == 0:
            weight_copies[2 * CHUNKS].wait()
        if t == query_tiles // 2:
            weight_copies[2 * CHUNKS + 1].wait()
        for n in range(out_tiles):
            out_acc[n] = out_term(t, n) if t == 0 else out_acc[n] + out_term(t, n)
    wait_mixed(query_tiles - 1)

    oa_copies, ob_copies = [], []

    def out_project(n):
        value = out_acc[n] + out_term(query_tiles - 1, n)
        for r in range(side):
            out_part[n, r % 2, r // 2] = value[r * rows : (r + 1) * rows]
        copy = pltpu.make_async_remote_copy(
            src_ref=out_part.at[n, 1 - core], dst_ref=out_recv_a.at[n],
            send_sem=oa_send.at[n], recv_sem=oa_recv.at[n], device_id=mate, device_id_type=MESH,
        )
        copy.start()
        oa_copies.append(copy)

    def out_pass_on(n):
        oa_copies[n].wait_recv()
        out_sum_b[n] = out_part[n, core, 1 - chip] + out_recv_a[n, 1 - chip]
        copy = pltpu.make_async_remote_copy(
            src_ref=out_sum_b.at[n], dst_ref=out_recv_b.at[n],
            send_sem=ob_send.at[n], recv_sem=ob_recv.at[n], device_id=across, device_id_type=MESH,
        )
        copy.start()
        ob_copies.append(copy)

    for n in range(out_tiles):
        out_project(n)
        if n > 1:
            out_pass_on(n - 2)
    for n in range(out_tiles - 2, out_tiles):
        out_pass_on(n)
    for n in range(out_tiles):
        ob_copies[n].wait_recv()
        out_ref[:, n * TILE : (n + 1) * TILE] = (
            out_part[n, core, chip] + out_recv_a[n, chip] + out_recv_b[n]
        ).astype(jnp.bfloat16)

    for c in range(CHUNKS):
        token_copy(c, 0, gx, outer).wait_send()
        token_copy(c, 1, gx, outer).wait_send()

        @pl.when(middle)
        def _():
            token_copy(c, 2, gx, outer).wait_send()
            token_copy(c, 3, far, outer).wait_send()

    for copy in stat_copies + a_copies + b_copies + oa_copies + ob_copies:
        copy.wait_send()
    for step, copy in mix_copies:
        if step == 0:
            pl.when(gx != gy)(copy.wait_send)
        else:
            copy.wait_send()


def fused_on_device(tokens, norm_gain, w_query, keyvalue_weight, w_out, segment_ids):
    rows, width = tokens.shape
    side = lax.axis_size("gx")
    query_tiles = w_query.shape[1] // TILE
    tiles = query_tiles + 1
    out_tiles = w_out.shape[1] // TILE
    f32, bf16 = jnp.float32, jnp.bfloat16
    dma = pltpu.SemaphoreType.DMA
    vmem = pl.BlockSpec(memory_space=pltpu.VMEM)
    hbm = pl.BlockSpec(memory_space=pl.ANY)
    return pl.pallas_call(
        fused_kernel,
        out_shape=jax.ShapeDtypeStruct((rows, w_out.shape[1]), bf16),
        in_specs=[hbm] * 6,
        out_specs=vmem,
        scratch_shapes=[
            pltpu.VMEM((1, width), f32),
            pltpu.VMEM(segment_ids.shape, jnp.int32),
            pltpu.VMEM((CHUNKS, side, rows, width // CHUNKS), bf16),
            pltpu.VMEM((side * side, 8, 128), f32),
            pltpu.VMEM((CHUNKS, side, rows, width // CHUNKS), bf16),
            pltpu.VMEM(w_query.shape, bf16),
            pltpu.VMEM(keyvalue_weight.shape, bf16),
            pltpu.VMEM(w_out.shape, bf16),
            pltpu.VMEM((tiles, 2, 2, rows, TILE), f32),
            pltpu.VMEM((tiles, 2, rows, TILE), f32),
            pltpu.VMEM((tiles, rows, TILE), f32),
            pltpu.VMEM((tiles, rows, TILE), f32),
            pltpu.VMEM((tiles, rows, TILE), f32),
            pltpu.VMEM((query_tiles, rows, TILE), bf16),
            pltpu.VMEM((query_tiles, side, rows, TILE), bf16),
            pltpu.VMEM((out_tiles, side * rows, TILE), f32),
            pltpu.VMEM((out_tiles, 2, 2, rows, TILE), f32),
            pltpu.VMEM((out_tiles, 2, rows, TILE), f32),
            pltpu.VMEM((out_tiles, rows, TILE), f32),
            pltpu.VMEM((out_tiles, rows, TILE), f32),
            dma((2 + CHUNKS,)), dma((2 * CHUNKS + 2,)),
            dma((CHUNKS, side)), dma((CHUNKS, side)),
            dma((side * side - 1,)), dma((side * side - 1,)),
            dma((tiles,)), dma((tiles,)), dma((tiles,)), dma((tiles,)),
            dma((query_tiles, side)), dma((query_tiles, side)),
            dma((out_tiles,)), dma((out_tiles,)), dma((out_tiles,)), dma((out_tiles,)),
        ],
        compiler_params=pltpu.CompilerParams(
            collective_id=0, has_side_effects=True, vmem_limit_bytes=63 * 1024 * 1024
        ),
        cost_estimate=pl.CostEstimate(
            flops=2 * side * rows * width * (w_query.shape[1] * 2 + keyvalue_weight.shape[1]),
            bytes_accessed=2 * (w_query.size + keyvalue_weight.size + w_out.size),
            transcendentals=0,
        ),
    )(tokens, norm_gain[None, :], segment_ids, w_query, keyvalue_weight, w_out)


def program_for(mesh):
    if mesh.shape["gx"] == 4 and mesh.shape["gy"] == 4:
        return fused_on_device
    return on_device


def solution(mesh):
    return jax.shard_map(
        program_for(mesh),
        mesh=mesh,
        in_specs=(
            P(("groups", "gx"), "gy"),
            P("gy"),
            P("gy", "gx"),
            P("gy", "gx"),
            P("gy", "gx"),
            P(("groups", "gx"), None),
        ),
        out_specs=P(("groups", "gy"), "gx"),
        check_vma=False,
    )
```

```python
import math

import jax
import jax.numpy as jnp
from jax import lax
from jax.experimental import pallas as pl
from jax.experimental.pallas import tpu as pltpu
from jax.sharding import PartitionSpec as P

MODEL_WIDTH = 8192
QUERY_HEADS = 64
KEYVALUE_HEADS = 8
HEAD_WIDTH = 128
SEGS = 3


EPSILON = 1e-05
ROPE_BASE = 500000.0
MASK_VALUE = -1e30


def row_positions(segments, segment_total):
    bounds = jnp.arange(segment_total + 1, dtype=jnp.int32)
    first_rows = jnp.sum((segments[:, None, :] < bounds[None, :, None]).astype(jnp.int32), axis=2)
    matches = segments[:, :, None] == bounds[None, None, :segment_total]
    segment_first = jnp.sum(jnp.where(matches, first_rows[:, None, :segment_total], 0), axis=2)
    context_length = first_rows[:, 1:2]
    row_index = jnp.arange(segments.shape[1], dtype=jnp.int32)[None, :]
    positions = jnp.where(segments == 0, row_index, context_length + row_index - segment_first)
    return positions.reshape(-1)


def rotate(values, positions):
    half_size = values.shape[-1] // 2
    frequency = ROPE_BASE ** (-2.0 * jnp.arange(half_size, dtype=jnp.float32) / values.shape[-1])
    angle = positions.astype(jnp.float32)[:, None, None] * frequency[None, None, :]
    cosine = jnp.cos(angle)
    sine = jnp.sin(angle)
    first_half = values[..., :half_size]
    second_half = values[..., half_size:]
    return jnp.concatenate(
        [first_half * cosine - second_half * sine, second_half * cosine + first_half * sine],
        axis=-1,
    )


def request_mask(segments):
    row_index = jnp.arange(segments.shape[0], dtype=jnp.int32)
    causal = row_index[None, :] <= row_index[:, None]
    same_part = (segments[None, :] == segments[:, None]) | (segments[None, :] == 0)
    return causal & same_part


def on_device(tokens, norm_gain, w_query, keyvalue_weight, w_out, segment_ids):
    column_group_count = lax.axis_size("gy")
    gy_index = lax.axis_index("gy")
    rows_here = tokens.shape[0]
    query_cols = w_query.shape[1]
    head_block = QUERY_HEADS // column_group_count
    keyvalue_block = KEYVALUE_HEADS // column_group_count
    group_width = QUERY_HEADS // KEYVALUE_HEADS
    query_width = head_block * HEAD_WIDTH
    keyval_width = keyvalue_block * 2 * HEAD_WIDTH
    local_positions = row_positions(segment_ids, SEGS)
    widened = tokens.astype(jnp.float32)
    squares = lax.psum(jnp.sum(widened * widened, axis=1), "gy")
    widened = tokens.astype(jnp.float32)
    normalized_input = (
        widened * lax.rsqrt(squares / MODEL_WIDTH + EPSILON)[:, None] * norm_gain[None, :]
    ).astype(jnp.bfloat16)
    piece_rows = lax.all_gather(normalized_input, "gx", axis=0, tiled=True)
    partial_heads = jnp.concatenate(
        [
            jnp.dot(piece_rows, w_query, preferred_element_type=jnp.float32),
            jnp.dot(piece_rows, keyvalue_weight, preferred_element_type=jnp.float32),
        ],
        axis=1,
    )
    query_part = partial_heads[:, :query_cols]
    keyval_part = partial_heads[:, query_cols:]
    query_sum, keyval_sum = lax.psum((query_part, keyval_part), "gy")
    query_rows, keyval_rows = (
        lax.all_to_all(query_sum, "gx", split_axis=0, concat_axis=1, tiled=True),
        lax.all_to_all(keyval_sum, "gx", split_axis=0, concat_axis=1, tiled=True),
    )
    query_here = lax.dynamic_slice_in_dim(query_rows, gy_index * query_width, query_width, 1)
    keyval_here = lax.dynamic_slice_in_dim(keyval_rows, gy_index * keyval_width, keyval_width, 1)
    heads_of_query = rotate(
        query_here.reshape(rows_here, head_block, HEAD_WIDTH), local_positions
    ).astype(jnp.bfloat16)
    heads_of_query = heads_of_query.reshape(rows_here, keyvalue_block, group_width, HEAD_WIDTH)
    keyvalue_pairs = keyval_here.reshape(rows_here, keyvalue_block, 2, HEAD_WIDTH)
    key_heads = rotate(keyvalue_pairs[:, :, 0], local_positions).astype(jnp.bfloat16)
    value_heads = keyvalue_pairs[:, :, 1].astype(jnp.bfloat16)
    score_scale = HEAD_WIDTH ** (-0.5)
    scores = (
        jnp.einsum("rkgd,tkd->kgrt", heads_of_query, key_heads, preferred_element_type=jnp.float32)
        * score_scale
    )
    visible = request_mask(segment_ids[0])
    scores = jnp.where(visible[None, None], scores, MASK_VALUE)
    row_top = jnp.max(scores, axis=-1, keepdims=True)
    weights = jnp.exp(scores - row_top)
    probabilities = (weights / jnp.sum(weights, axis=-1, keepdims=True)).astype(jnp.bfloat16)
    mixed_heads = jnp.einsum(
        "kgrt,tkd->rkgd", probabilities, value_heads, preferred_element_type=jnp.float32
    )
    mixed = mixed_heads.astype(jnp.bfloat16).reshape(rows_here, query_width)
    output_terms = jnp.dot(
        lax.all_gather(mixed, "gx", axis=0, tiled=True), w_out, preferred_element_type=jnp.float32
    )
    return lax.psum_scatter(output_terms, "gy", scatter_dimension=0, tiled=True).astype(
        jnp.bfloat16
    )


MESH = pl.DeviceIdType.MESH
TILE = 512
CHUNKS = 2


def fused_kernel(
    tokens_ref, gain_hbm, segments_hbm, wq_ref, wkv_ref, wo_ref, out_ref,
    gain_ref, segments_ref, tok_all, stats, normed, wq, wkv, wo, part, recv_a, sum_b, recv_b, final, mixed_send, mixed_all,
    out_acc, out_part, out_recv_a, out_sum_b, out_recv_b,
    first_recv, first_sem, out_first_recv, out_first_sem,
    local_sem, weight_sem,
    tok_send, tok_recv, stat_send, stat_recv,
    a_send, a_recv, b_send, b_recv, mix_send, mix_recv,
    oa_send, oa_recv, ob_send, ob_recv,
):
    side = 4
    gx = lax.axis_index("gx")
    gy = lax.axis_index("gy")
    chip, core = gy // 2, gy % 2
    me = gx * side + gy
    mate = {"gx": gx, "gy": chip * 2 + (1 - core)}
    across = {"gx": gx, "gy": (1 - chip) * 2 + core}
    rows = tok_all.shape[2]
    span = tok_all.shape[3]
    query_tiles = wq_ref.shape[1] // TILE
    tiles = query_tiles + 1

    own_tokens = [
        pltpu.make_async_copy(
            tokens_ref.at[:, pl.ds(c * span, span)], tok_all.at[c, gx], local_sem.at[2 + c]
        )
        for c in range(CHUNKS)
    ]
    for copy in own_tokens:
        copy.start()
    own_segments = pltpu.make_async_copy(segments_hbm, segments_ref, local_sem.at[0])
    own_segments.start()
    own_gain = pltpu.make_async_copy(gain_hbm, gain_ref, local_sem.at[1])
    own_gain.start()
    weight_copies = []
    for c in range(CHUNKS):
        piece = pl.ds(c * span, span)
        weight_copies.append(
            pltpu.make_async_copy(wkv_ref.at[piece, :], wkv.at[piece, :], weight_sem.at[2 * c])
        )
        weight_copies.append(
            pltpu.make_async_copy(wq_ref.at[piece, :], wq.at[piece, :], weight_sem.at[2 * c + 1])
        )
    half = wo_ref.shape[0] // 2
    for j in range(2):
        piece = pl.ds(j * half, half)
        weight_copies.append(
            pltpu.make_async_copy(wo_ref.at[piece, :], wo.at[piece, :], weight_sem.at[2 * CHUNKS + j])
        )
    for copy in weight_copies[: 2 * CHUNKS]:
        copy.start()

    barrier = pltpu.get_barrier_semaphore()
    for step in range(1, side * side):
        peer = (me + step) % (side * side)
        pl.semaphore_signal(
            barrier, inc=1, device_id={"gx": peer // side, "gy": peer % side}, device_id_type=MESH
        )
    square_sum = jnp.zeros((rows, 1), jnp.float32)
    for c in range(CHUNKS):
        own_tokens[c].wait()
        mine = tok_all[c, gx].astype(jnp.float32)
        square_sum += jnp.sum(mine * mine, axis=1, keepdims=True)
    row_id = lax.broadcasted_iota(jnp.int32, (rows, 128), 0)
    col_id = lax.broadcasted_iota(jnp.int32, (rows, 128), 1)
    diagonal = row_id == col_id
    stats[me] = jnp.zeros(stats.shape[1:], jnp.float32)
    stats[me, 0:1, :] = jnp.sum(jnp.where(diagonal, square_sum, 0.0), axis=0, keepdims=True)
    own_segments.wait()
    stats[me, 1:2, 0:rows] = segments_ref[...].astype(jnp.float32)
    half_index = (col_id % (HEAD_WIDTH // 2)).astype(jnp.float32)
    table_angle = row_id.astype(jnp.float32) * jnp.exp(
        half_index * (-2.0 * math.log(ROPE_BASE) / HEAD_WIDTH)
    )
    cosine_table = jnp.cos(table_angle)
    sine_table = jnp.sin(table_angle)
    sine_table = jnp.where(col_id < HEAD_WIDTH // 2, -sine_table, sine_table)
    pl.semaphore_wait(barrier, side * side - 1)

    stat_copies = []
    for step in range(1, side * side):
        peer = (me + step) % (side * side)
        copy = pltpu.make_async_remote_copy(
            src_ref=stats.at[me], dst_ref=stats.at[me],
            send_sem=stat_send.at[step - 1], recv_sem=stat_recv.at[step - 1],
            device_id={"gx": peer // side, "gy": peer % side}, device_id_type=MESH,
        )
        copy.start()
        stat_copies.append(copy)
    middle = (gx == 1) | (gx == 2)
    outer = 3 * (gx // 2)
    far = 3 - outer

    def token_copy(c, slot, block, target):
        return pltpu.make_async_remote_copy(
            src_ref=tok_all.at[c, block], dst_ref=tok_all.at[c, block],
            send_sem=tok_send.at[c, slot], recv_sem=tok_recv.at[c, block],
            device_id={"gx": target, "gy": gy}, device_id_type=MESH,
        )

    for c in range(CHUNKS):
        token_copy(c, 1, gx, (gx + 2) % side).start()
        token_copy(c, 0, gx, 1 + gx % 2).start()
        pl.when(middle)(token_copy(c, 2, gx, outer).start)
    for copy in weight_copies[2 * CHUNKS :]:
        copy.start()

    def hand_on(c):
        @pl.when(middle)
        def _():
            copy = token_copy(c, 3, far, outer)
            copy.wait_recv()
            copy.start()

    for copy in stat_copies:
        copy.wait_recv()

    def as_column(row):
        return jnp.sum(jnp.where(diagonal, row, 0.0), axis=1, keepdims=True)

    segment_row = stats[gy * side + gy, 1:2, :]
    segment_col = as_column(segment_row)
    in_request = col_id < rows
    context = jnp.sum(
        jnp.where(in_request & (segment_row < 0.5), 1.0, 0.0), axis=1, keepdims=True
    )
    first = jnp.sum(
        jnp.where(in_request & (segment_row < segment_col), 1.0, 0.0), axis=1, keepdims=True
    )
    index = row_id[:, 0:1].astype(jnp.float32)
    position = jnp.where(segment_col < 0.5, index, context + index - first)
    cosine = jnp.zeros((rows, HEAD_WIDTH), jnp.float32)
    sine = jnp.zeros((rows, HEAD_WIDTH), jnp.float32)
    for p in range(rows):
        here = position == float(p)
        cosine = jnp.where(here, cosine_table[p : p + 1], cosine)
        sine = jnp.where(here, sine_table[p : p + 1], sine)
    visible = (col_id <= row_id) & ((segment_row == segment_col) | (segment_row < 0.5))
    visible = jnp.where(visible, 1.0, 0.0)[:, :rows]
    group_width = QUERY_HEADS // KEYVALUE_HEADS
    visible_all = jnp.concatenate([visible] * (TILE // HEAD_WIDTH), axis=0) > 0.5

    own_gain.wait()
    scales = []
    for block in range(side):
        total = stats[block * side, 0:1, :]
        for k in range(1, side):
            total = total + stats[block * side + k, 0:1, :]
        scales.append(lax.rsqrt(as_column(total) / MODEL_WIDTH + EPSILON))

    def rotated(values):
        return (values * cosine + pltpu.roll(values, HEAD_WIDTH // 2, 1) * sine).astype(
            jnp.bfloat16
        )

    a_copies, b_copies, first_copies = [None], [None], []

    def normalize(c):
        for step in (1, 3, 2):
            copy = token_copy(c, 0, (gx + step) % side, outer)
            if step == 2:
                pl.when(jnp.logical_not(middle))(copy.wait_recv)
            else:
                copy.wait_recv()
        gain = gain_ref[:, c * span : (c + 1) * span]
        for block in range(side):
            normed[c, block] = (
                tok_all[c, block].astype(jnp.float32) * scales[block] * gain
            ).astype(jnp.bfloat16)
        weight_copies[2 * c].wait()
        weight_copies[2 * c + 1].wait()

    def project(c, n):
        piece = slice(c * span, (c + 1) * span)
        weights = wkv[piece, :] if n == 0 else wq[piece, (n - 1) * TILE : n * TILE]
        value = jnp.dot(
            normed[c].reshape(side * rows, span), weights, preferred_element_type=jnp.float32
        )
        for r in range(side):
            term = value[r * rows : (r + 1) * rows]
            part[n, r % 2, r // 2] = term if c == 0 else part[n, r % 2, r // 2] + term

    diagonal_peer = {"gx": gx, "gy": (1 - chip) * 2 + (1 - core)}
    owners = [(mate, 1 - core, chip), (across, core, 1 - chip), (diagonal_peer, 1 - core, 1 - chip)]

    def give_owners(source, landing, send_sem, recv_sem):
        copies = []
        for k in (1, 2, 0):
            peer, peer_core, peer_chip = owners[k]
            copy = pltpu.make_async_remote_copy(
                src_ref=source.at[peer_core, peer_chip], dst_ref=landing.at[k],
                send_sem=send_sem.at[k], recv_sem=recv_sem.at[k],
                device_id=peer, device_id_type=MESH,
            )
            copy.start()
            copies.append(copy)
        return copies

    def give_mate(n):
        copy = pltpu.make_async_remote_copy(
            src_ref=part.at[n, 1 - core], dst_ref=recv_a.at[n],
            send_sem=a_send.at[n], recv_sem=a_recv.at[n], device_id=mate, device_id_type=MESH,
        )
        copy.start()
        a_copies.append(copy)

    def pass_on(n):
        a_copies[n].wait_recv()
        sum_b[n] = part[n, core, 1 - chip] + recv_a[n, 1 - chip]
        copy = pltpu.make_async_remote_copy(
            src_ref=sum_b.at[n], dst_ref=recv_b.at[n],
            send_sem=b_send.at[n], recv_sem=b_recv.at[n], device_id=across, device_id_type=MESH,
        )
        copy.start()
        b_copies.append(copy)

    def finish(n):
        if n == 0:
            for copy in first_copies:
                copy.wait_recv()
            return part[0, core, chip] + first_recv[0] + (first_recv[1] + first_recv[2])
        b_copies[n].wait_recv()
        return part[n, core, chip] + recv_a[n, chip] + recv_b[n]

    hand_on(0)
    for c in range(CHUNKS - 1):
        hand_on(c + 1)
        normalize(c)
        for n in range(tiles):
            project(c, n)
    normalize(CHUNKS - 1)
    for n in range(tiles):
        project(CHUNKS - 1, n)
        if n == 0:
            first_copies.extend(give_owners(part.at[0], first_recv, first_sem.at[0], first_sem.at[1]))
        else:
            give_mate(n)
        if n > 3:
            pass_on(n - 3)
    for n in range(tiles - 3, tiles):
        pass_on(n)

    heads_in_tile = TILE // HEAD_WIDTH
    keyval = finish(0)
    mix_copies = []
    key_head = value_head = None
    for t in range(query_tiles):
        if t * heads_in_tile % group_width == 0:
            j = t * heads_in_tile // group_width
            key_head = rotated(keyval[:, 2 * j * HEAD_WIDTH : (2 * j + 1) * HEAD_WIDTH])
            value_head = keyval[:, (2 * j + 1) * HEAD_WIDTH : (2 * j + 2) * HEAD_WIDTH].astype(
                jnp.bfloat16
            )
        query_tile = finish(1 + t)
        query = jnp.concatenate(
            [
                rotated(query_tile[:, h * HEAD_WIDTH : (h + 1) * HEAD_WIDTH])
                for h in range(heads_in_tile)
            ],
            axis=0,
        )
        scores = lax.dot_general(
            query, key_head, (((1,), (1,)), ((), ())), preferred_element_type=jnp.float32
        ) * (HEAD_WIDTH ** (-0.5))
        scores = jnp.where(visible_all, scores, MASK_VALUE)
        weights = jnp.exp(scores - jnp.max(scores, axis=1, keepdims=True))
        probs = (weights / jnp.sum(weights, axis=1, keepdims=True)).astype(jnp.bfloat16)
        mixed = jnp.dot(probs, value_head, preferred_element_type=jnp.float32).astype(jnp.bfloat16)
        for h in range(heads_in_tile):
            mixed_send[t, :, h * HEAD_WIDTH : (h + 1) * HEAD_WIDTH] = mixed[
                h * rows : (h + 1) * rows
            ]

        @pl.when(gx == gy)
        def _():
            mixed_all[t, gy] = mixed_send[t]

        for step in (3, 2, 1, 0):
            copy = pltpu.make_async_remote_copy(
                src_ref=mixed_send.at[t], dst_ref=mixed_all.at[t, gy],
                send_sem=mix_send.at[t, step], recv_sem=mix_recv.at[t, gy],
                device_id={"gx": (gx + step) % side, "gy": gx}, device_id_type=MESH,
            )
            if step == 0:
                pl.when(gx != gy)(copy.start)
            else:
                copy.start()
            mix_copies.append((step, copy))

    def wait_mixed(t):
        for step in range(side):
            r = (gy + step) % side
            copy = pltpu.make_async_remote_copy(
                src_ref=mixed_send.at[t], dst_ref=mixed_all.at[t, r],
                send_sem=mix_send.at[t, 0], recv_sem=mix_recv.at[t, r],
                device_id=mate, device_id_type=MESH,
            )
            if step == 0:
                pl.when(gx != gy)(copy.wait_recv)
            else:
                copy.wait_recv()

    out_tiles = wo_ref.shape[1] // TILE

    def out_term(t, n):
        return jnp.dot(
            mixed_all[t].reshape(side * rows, TILE),
            wo[t * TILE : (t + 1) * TILE, n * TILE : (n + 1) * TILE],
            preferred_element_type=jnp.float32,
        )

    for t in range(query_tiles - 1):
        wait_mixed(t)
        if t == 0:
            weight_copies[2 * CHUNKS].wait()
        if t == query_tiles // 2:
            weight_copies[2 * CHUNKS + 1].wait()
        for n in range(out_tiles):
            out_acc[n] = out_term(t, n) if t == 0 else out_acc[n] + out_term(t, n)
    wait_mixed(query_tiles - 1)

    oa_copies, ob_copies, out_first_copies = [], [], []

    def out_project(n):
        value = out_acc[n] + out_term(query_tiles - 1, n)
        for r in range(side):
            out_part[n, r % 2, r // 2] = value[r * rows : (r + 1) * rows]
        if n == 0:
            out_first_copies.extend(
                give_owners(out_part.at[0], out_first_recv, out_first_sem.at[0], out_first_sem.at[1])
            )
            oa_copies.append(None)
            ob_copies.append(None)
            return
        copy = pltpu.make_async_remote_copy(
            src_ref=out_part.at[n, 1 - core], dst_ref=out_recv_a.at[n],
            send_sem=oa_send.at[n], recv_sem=oa_recv.at[n], device_id=mate, device_id_type=MESH,
        )
        copy.start()
        oa_copies.append(copy)

    def out_pass_on(n):
        oa_copies[n].wait_recv()
        out_sum_b[n] = out_part[n, core, 1 - chip] + out_recv_a[n, 1 - chip]
        copy = pltpu.make_async_remote_copy(
            src_ref=out_sum_b.at[n], dst_ref=out_recv_b.at[n],
            send_sem=ob_send.at[n], recv_sem=ob_recv.at[n], device_id=across, device_id_type=MESH,
        )
        copy.start()
        ob_copies.append(copy)

    for n in range(out_tiles):
        out_project(n)
        if n > 2:
            out_pass_on(n - 2)
    for n in range(out_tiles - 2, out_tiles):
        out_pass_on(n)
    for copy in out_first_copies:
        copy.wait_recv()
    out_ref[:, 0:TILE] = (
        out_part[0, core, chip] + out_first_recv[0] + (out_first_recv[1] + out_first_recv[2])
    ).astype(jnp.bfloat16)
    for n in range(1, out_tiles):
        ob_copies[n].wait_recv()
        out_ref[:, n * TILE : (n + 1) * TILE] = (
            out_part[n, core, chip] + out_recv_a[n, chip] + out_recv_b[n]
        ).astype(jnp.bfloat16)

    for c in range(CHUNKS):
        token_copy(c, 0, gx, outer).wait_send()
        token_copy(c, 1, gx, outer).wait_send()

        @pl.when(middle)
        def _():
            token_copy(c, 2, gx, outer).wait_send()
            token_copy(c, 3, far, outer).wait_send()

    for copy in stat_copies + first_copies + a_copies[1:] + b_copies[1:]:
        copy.wait_send()
    for copy in out_first_copies + oa_copies[1:] + ob_copies[1:]:
        copy.wait_send()
    for step, copy in mix_copies:
        if step == 0:
            pl.when(gx != gy)(copy.wait_send)
        else:
            copy.wait_send()


def fused_on_device(tokens, norm_gain, w_query, keyvalue_weight, w_out, segment_ids):
    rows, width = tokens.shape
    side = lax.axis_size("gx")
    query_tiles = w_query.shape[1] // TILE
    tiles = query_tiles + 1
    out_tiles = w_out.shape[1] // TILE
    f32, bf16 = jnp.float32, jnp.bfloat16
    dma = pltpu.SemaphoreType.DMA
    vmem = pl.BlockSpec(memory_space=pltpu.VMEM)
    hbm = pl.BlockSpec(memory_space=pl.ANY)
    return pl.pallas_call(
        fused_kernel,
        out_shape=jax.ShapeDtypeStruct((rows, w_out.shape[1]), bf16),
        in_specs=[hbm] * 6,
        out_specs=vmem,
        scratch_shapes=[
            pltpu.VMEM((1, width), f32),
            pltpu.VMEM(segment_ids.shape, jnp.int32),
            pltpu.VMEM((CHUNKS, side, rows, width // CHUNKS), bf16),
            pltpu.VMEM((side * side, 2, 128), f32),
            pltpu.VMEM((CHUNKS, side, rows, width // CHUNKS), bf16),
            pltpu.VMEM(w_query.shape, bf16),
            pltpu.VMEM(keyvalue_weight.shape, bf16),
            pltpu.VMEM(w_out.shape, bf16),
            pltpu.VMEM((tiles, 2, 2, rows, TILE), f32),
            pltpu.VMEM((tiles, 2, rows, TILE), f32),
            pltpu.VMEM((tiles, rows, TILE), f32),
            pltpu.VMEM((tiles, rows, TILE), f32),
            pltpu.VMEM((tiles, rows, TILE), f32),
            pltpu.VMEM((query_tiles, rows, TILE), bf16),
            pltpu.VMEM((query_tiles, side, rows, TILE), bf16),
            pltpu.VMEM((out_tiles, side * rows, TILE), f32),
            pltpu.VMEM((out_tiles, 2, 2, rows, TILE), f32),
            pltpu.VMEM((out_tiles, 2, rows, TILE), f32),
            pltpu.VMEM((out_tiles, rows, TILE), f32),
            pltpu.VMEM((out_tiles, rows, TILE), f32),
            pltpu.VMEM((3, rows, TILE), f32),
            dma((2, 3)),
            pltpu.VMEM((3, rows, TILE), f32),
            dma((2, 3)),
            dma((2 + CHUNKS,)), dma((2 * CHUNKS + 2,)),
            dma((CHUNKS, side)), dma((CHUNKS, side)),
            dma((side * side - 1,)), dma((side * side - 1,)),
            dma((tiles,)), dma((tiles,)), dma((tiles,)), dma((tiles,)),
            dma((query_tiles, side)), dma((query_tiles, side)),
            dma((out_tiles,)), dma((out_tiles,)), dma((out_tiles,)), dma((out_tiles,)),
        ],
        compiler_params=pltpu.CompilerParams(
            collective_id=0, has_side_effects=True, vmem_limit_bytes=63 * 1024 * 1024
        ),
        cost_estimate=pl.CostEstimate(
            flops=2 * side * rows * width * (w_query.shape[1] * 2 + keyvalue_weight.shape[1]),
            bytes_accessed=2 * (w_query.size + keyvalue_weight.size + w_out.size),
            transcendentals=0,
        ),
    )(tokens, norm_gain[None, :], segment_ids, w_query, keyvalue_weight, w_out)


def program_for(mesh):
    if mesh.shape["gx"] == 4 and mesh.shape["gy"] == 4:
        return fused_on_device
    return on_device


def solution(mesh):
    return jax.shard_map(
        program_for(mesh),
        mesh=mesh,
        in_specs=(
            P(("groups", "gx"), "gy"),
            P("gy"),
            P("gy", "gx"),
            P("gy", "gx"),
            P("gy", "gx"),
            P(("groups", "gx"), None),
        ),
        out_specs=P(("groups", "gy"), "gx"),
        check_vma=False,
    )
```

```python
import math

import jax
import jax.numpy as jnp
from jax import lax
from jax.experimental import pallas as pl
from jax.experimental.pallas import tpu as pltpu
from jax.sharding import PartitionSpec as P

MODEL_WIDTH = 8192
QUERY_HEADS = 64
KEYVALUE_HEADS = 8
HEAD_WIDTH = 128
SEGS = 3


EPSILON = 1e-05
ROPE_BASE = 500000.0
MASK_VALUE = -1e30


def row_positions(segments, segment_total):
    bounds = jnp.arange(segment_total + 1, dtype=jnp.int32)
    first_rows = jnp.sum((segments[:, None, :] < bounds[None, :, None]).astype(jnp.int32), axis=2)
    matches = segments[:, :, None] == bounds[None, None, :segment_total]
    segment_first = jnp.sum(jnp.where(matches, first_rows[:, None, :segment_total], 0), axis=2)
    context_length = first_rows[:, 1:2]
    row_index = jnp.arange(segments.shape[1], dtype=jnp.int32)[None, :]
    positions = jnp.where(segments == 0, row_index, context_length + row_index - segment_first)
    return positions.reshape(-1)


def rotate(values, positions):
    half_size = values.shape[-1] // 2
    frequency = ROPE_BASE ** (-2.0 * jnp.arange(half_size, dtype=jnp.float32) / values.shape[-1])
    angle = positions.astype(jnp.float32)[:, None, None] * frequency[None, None, :]
    cosine = jnp.cos(angle)
    sine = jnp.sin(angle)
    first_half = values[..., :half_size]
    second_half = values[..., half_size:]
    return jnp.concatenate(
        [first_half * cosine - second_half * sine, second_half * cosine + first_half * sine],
        axis=-1,
    )


def request_mask(segments):
    row_index = jnp.arange(segments.shape[0], dtype=jnp.int32)
    causal = row_index[None, :] <= row_index[:, None]
    same_part = (segments[None, :] == segments[:, None]) | (segments[None, :] == 0)
    return causal & same_part


def on_device(tokens, norm_gain, w_query, keyvalue_weight, w_out, segment_ids):
    column_group_count = lax.axis_size("gy")
    gy_index = lax.axis_index("gy")
    rows_here = tokens.shape[0]
    query_cols = w_query.shape[1]
    head_block = QUERY_HEADS // column_group_count
    keyvalue_block = KEYVALUE_HEADS // column_group_count
    group_width = QUERY_HEADS // KEYVALUE_HEADS
    query_width = head_block * HEAD_WIDTH
    keyval_width = keyvalue_block * 2 * HEAD_WIDTH
    local_positions = row_positions(segment_ids, SEGS)
    widened = tokens.astype(jnp.float32)
    squares = lax.psum(jnp.sum(widened * widened, axis=1), "gy")
    widened = tokens.astype(jnp.float32)
    normalized_input = (
        widened * lax.rsqrt(squares / MODEL_WIDTH + EPSILON)[:, None] * norm_gain[None, :]
    ).astype(jnp.bfloat16)
    piece_rows = lax.all_gather(normalized_input, "gx", axis=0, tiled=True)
    partial_heads = jnp.concatenate(
        [
            jnp.dot(piece_rows, w_query, preferred_element_type=jnp.float32),
            jnp.dot(piece_rows, keyvalue_weight, preferred_element_type=jnp.float32),
        ],
        axis=1,
    )
    query_part = partial_heads[:, :query_cols]
    keyval_part = partial_heads[:, query_cols:]
    query_sum, keyval_sum = lax.psum((query_part, keyval_part), "gy")
    query_rows, keyval_rows = (
        lax.all_to_all(query_sum, "gx", split_axis=0, concat_axis=1, tiled=True),
        lax.all_to_all(keyval_sum, "gx", split_axis=0, concat_axis=1, tiled=True),
    )
    query_here = lax.dynamic_slice_in_dim(query_rows, gy_index * query_width, query_width, 1)
    keyval_here = lax.dynamic_slice_in_dim(keyval_rows, gy_index * keyval_width, keyval_width, 1)
    heads_of_query = rotate(
        query_here.reshape(rows_here, head_block, HEAD_WIDTH), local_positions
    ).astype(jnp.bfloat16)
    heads_of_query = heads_of_query.reshape(rows_here, keyvalue_block, group_width, HEAD_WIDTH)
    keyvalue_pairs = keyval_here.reshape(rows_here, keyvalue_block, 2, HEAD_WIDTH)
    key_heads = rotate(keyvalue_pairs[:, :, 0], local_positions).astype(jnp.bfloat16)
    value_heads = keyvalue_pairs[:, :, 1].astype(jnp.bfloat16)
    score_scale = HEAD_WIDTH ** (-0.5)
    scores = (
        jnp.einsum("rkgd,tkd->kgrt", heads_of_query, key_heads, preferred_element_type=jnp.float32)
        * score_scale
    )
    visible = request_mask(segment_ids[0])
    scores = jnp.where(visible[None, None], scores, MASK_VALUE)
    row_top = jnp.max(scores, axis=-1, keepdims=True)
    weights = jnp.exp(scores - row_top)
    probabilities = (weights / jnp.sum(weights, axis=-1, keepdims=True)).astype(jnp.bfloat16)
    mixed_heads = jnp.einsum(
        "kgrt,tkd->rkgd", probabilities, value_heads, preferred_element_type=jnp.float32
    )
    mixed = mixed_heads.astype(jnp.bfloat16).reshape(rows_here, query_width)
    output_terms = jnp.dot(
        lax.all_gather(mixed, "gx", axis=0, tiled=True), w_out, preferred_element_type=jnp.float32
    )
    return lax.psum_scatter(output_terms, "gy", scatter_dimension=0, tiled=True).astype(
        jnp.bfloat16
    )


MESH = pl.DeviceIdType.MESH
TILE = 512
CHUNKS = 2


def fused_kernel(
    tokens_ref, gain_hbm, segments_hbm, wq_ref, wkv_ref, wo_ref, out_ref,
    gain_ref, segments_ref, tok_all, stats, normed, wq, wkv, wo, part, recv_a, sum_b, recv_b, final, mixed_send, mixed_all,
    out_acc, out_part, out_recv_a, out_sum_b, out_recv_b,
    first_recv, first_sem, out_first_recv, out_first_sem,
    local_sem, weight_sem,
    tok_send, tok_recv, stat_send, stat_recv,
    a_send, a_recv, b_send, b_recv, mix_send, mix_recv,
    oa_send, oa_recv, ob_send, ob_recv,
):
    side = 4
    gx = lax.axis_index("gx")
    gy = lax.axis_index("gy")
    chip, core = gy // 2, gy % 2
    me = gx * side + gy
    mate = {"gx": gx, "gy": chip * 2 + (1 - core)}
    across = {"gx": gx, "gy": (1 - chip) * 2 + core}
    rows = tok_all.shape[2]
    span = tok_all.shape[3]
    query_tiles = wq_ref.shape[1] // TILE
    tiles = query_tiles + 1

    own_tokens = [
        pltpu.make_async_copy(
            tokens_ref.at[:, pl.ds(c * span, span)], tok_all.at[c, gx], local_sem.at[2 + c]
        )
        for c in range(CHUNKS)
    ]
    for copy in own_tokens:
        copy.start()
    own_segments = pltpu.make_async_copy(segments_hbm, segments_ref, local_sem.at[0])
    own_segments.start()
    own_gain = pltpu.make_async_copy(gain_hbm, gain_ref, local_sem.at[1])
    own_gain.start()
    weight_copies = []
    for c in range(CHUNKS):
        piece = pl.ds(c * span, span)
        weight_copies.append(
            pltpu.make_async_copy(wkv_ref.at[piece, :], wkv.at[piece, :], weight_sem.at[2 * c])
        )
        weight_copies.append(
            pltpu.make_async_copy(wq_ref.at[piece, :], wq.at[piece, :], weight_sem.at[2 * c + 1])
        )
    half = wo_ref.shape[0] // 2
    for j in range(2):
        piece = pl.ds(j * half, half)
        weight_copies.append(
            pltpu.make_async_copy(wo_ref.at[piece, :], wo.at[piece, :], weight_sem.at[2 * CHUNKS + j])
        )
    for copy in weight_copies[: 2]:
        copy.start()

    barrier = pltpu.get_barrier_semaphore()
    for step in range(1, side * side):
        peer = (me + step) % (side * side)
        pl.semaphore_signal(
            barrier, inc=1, device_id={"gx": peer // side, "gy": peer % side}, device_id_type=MESH
        )
    square_sum = jnp.zeros((rows, 1), jnp.float32)
    for c in range(CHUNKS):
        own_tokens[c].wait()
        mine = tok_all[c, gx].astype(jnp.float32)
        square_sum += jnp.sum(mine * mine, axis=1, keepdims=True)
    row_id = lax.broadcasted_iota(jnp.int32, (rows, 128), 0)
    col_id = lax.broadcasted_iota(jnp.int32, (rows, 128), 1)
    diagonal = row_id == col_id
    stats[me] = jnp.zeros(stats.shape[1:], jnp.float32)
    stats[me, 0:1, :] = jnp.sum(jnp.where(diagonal, square_sum, 0.0), axis=0, keepdims=True)
    own_segments.wait()
    stats[me, 1:2, 0:rows] = segments_ref[...].astype(jnp.float32)
    half_index = (col_id % (HEAD_WIDTH // 2)).astype(jnp.float32)
    table_angle = row_id.astype(jnp.float32) * jnp.exp(
        half_index * (-2.0 * math.log(ROPE_BASE) / HEAD_WIDTH)
    )
    cosine_table = jnp.cos(table_angle)
    sine_table = jnp.sin(table_angle)
    sine_table = jnp.where(col_id < HEAD_WIDTH // 2, -sine_table, sine_table)
    pl.semaphore_wait(barrier, side * side - 1)

    stat_copies = []
    for step in range(1, side * side):
        peer = (me + step) % (side * side)
        copy = pltpu.make_async_remote_copy(
            src_ref=stats.at[me], dst_ref=stats.at[me],
            send_sem=stat_send.at[step - 1], recv_sem=stat_recv.at[step - 1],
            device_id={"gx": peer // side, "gy": peer % side}, device_id_type=MESH,
        )
        copy.start()
        stat_copies.append(copy)
    middle = (gx == 1) | (gx == 2)
    outer = 3 * (gx // 2)
    far = 3 - outer

    def token_copy(c, slot, block, target):
        return pltpu.make_async_remote_copy(
            src_ref=tok_all.at[c, block], dst_ref=tok_all.at[c, block],
            send_sem=tok_send.at[c, slot], recv_sem=tok_recv.at[c, block],
            device_id={"gx": target, "gy": gy}, device_id_type=MESH,
        )

    for c in range(CHUNKS):
        token_copy(c, 1, gx, (gx + 2) % side).start()
        token_copy(c, 0, gx, 1 + gx % 2).start()
        pl.when(middle)(token_copy(c, 2, gx, outer).start)
    for copy in weight_copies[2 :]:
        copy.start()

    def hand_on(c):
        @pl.when(middle)
        def _():
            copy = token_copy(c, 3, far, outer)
            copy.wait_recv()
            copy.start()

    for copy in stat_copies:
        copy.wait_recv()

    def as_column(row):
        return jnp.sum(jnp.where(diagonal, row, 0.0), axis=1, keepdims=True)

    segment_row = stats[gy * side + gy, 1:2, :]
    segment_col = as_column(segment_row)
    in_request = col_id < rows
    context = jnp.sum(
        jnp.where(in_request & (segment_row < 0.5), 1.0, 0.0), axis=1, keepdims=True
    )
    first = jnp.sum(
        jnp.where(in_request & (segment_row < segment_col), 1.0, 0.0), axis=1, keepdims=True
    )
    index = row_id[:, 0:1].astype(jnp.float32)
    position = jnp.where(segment_col < 0.5, index, context + index - first)
    cosine = jnp.zeros((rows, HEAD_WIDTH), jnp.float32)
    sine = jnp.zeros((rows, HEAD_WIDTH), jnp.float32)
    for p in range(rows):
        here = position == float(p)
        cosine = jnp.where(here, cosine_table[p : p + 1], cosine)
        sine = jnp.where(here, sine_table[p : p + 1], sine)
    visible = (col_id <= row_id) & ((segment_row == segment_col) | (segment_row < 0.5))
    visible = jnp.where(visible, 1.0, 0.0)[:, :rows]
    group_width = QUERY_HEADS // KEYVALUE_HEADS
    visible_all = jnp.concatenate([visible] * (TILE // HEAD_WIDTH), axis=0) > 0.5

    own_gain.wait()
    scales = []
    for block in range(side):
        total = stats[block * side, 0:1, :]
        for k in range(1, side):
            total = total + stats[block * side + k, 0:1, :]
        scales.append(lax.rsqrt(as_column(total) / MODEL_WIDTH + EPSILON))

    def rotated(values):
        return (values * cosine + pltpu.roll(values, HEAD_WIDTH // 2, 1) * sine).astype(
            jnp.bfloat16
        )

    a_copies, b_copies, first_copies = [None], [None], []

    def normalize(c):
        for step in (1, 3, 2):
            copy = token_copy(c, 0, (gx + step) % side, outer)
            if step == 2:
                pl.when(jnp.logical_not(middle))(copy.wait_recv)
            else:
                copy.wait_recv()
        gain = gain_ref[:, c * span : (c + 1) * span]
        for block in range(side):
            normed[c, block] = (
                tok_all[c, block].astype(jnp.float32) * scales[block] * gain
            ).astype(jnp.bfloat16)
        weight_copies[2 * c].wait()
        weight_copies[2 * c + 1].wait()

    def project(c, n):
        piece = slice(c * span, (c + 1) * span)
        weights = wkv[piece, :] if n == 0 else wq[piece, (n - 1) * TILE : n * TILE]
        value = jnp.dot(
            normed[c].reshape(side * rows, span), weights, preferred_element_type=jnp.float32
        )
        for r in range(side):
            term = value[r * rows : (r + 1) * rows]
            part[n, r % 2, r // 2] = term if c == 0 else part[n, r % 2, r // 2] + term

    diagonal_peer = {"gx": gx, "gy": (1 - chip) * 2 + (1 - core)}
    owners = [(mate, 1 - core, chip), (across, core, 1 - chip), (diagonal_peer, 1 - core, 1 - chip)]

    def give_owners(source, landing, send_sem, recv_sem):
        copies = []
        for k in (1, 2, 0):
            peer, peer_core, peer_chip = owners[k]
            copy = pltpu.make_async_remote_copy(
                src_ref=source.at[peer_core, peer_chip], dst_ref=landing.at[k],
                send_sem=send_sem.at[k], recv_sem=recv_sem.at[k],
                device_id=peer, device_id_type=MESH,
            )
            copy.start()
            copies.append(copy)
        return copies

    def give_mate(n):
        copy = pltpu.make_async_remote_copy(
            src_ref=part.at[n, 1 - core], dst_ref=recv_a.at[n],
            send_sem=a_send.at[n], recv_sem=a_recv.at[n], device_id=mate, device_id_type=MESH,
        )
        copy.start()
        a_copies.append(copy)

    def pass_on(n):
        a_copies[n].wait_recv()
        sum_b[n] = part[n, core, 1 - chip] + recv_a[n, 1 - chip]
        copy = pltpu.make_async_remote_copy(
            src_ref=sum_b.at[n], dst_ref=recv_b.at[n],
            send_sem=b_send.at[n], recv_sem=b_recv.at[n], device_id=across, device_id_type=MESH,
        )
        copy.start()
        b_copies.append(copy)

    def finish(n):
        if n == 0:
            for copy in first_copies:
                copy.wait_recv()
            return part[0, core, chip] + first_recv[0] + (first_recv[1] + first_recv[2])
        b_copies[n].wait_recv()
        return part[n, core, chip] + recv_a[n, chip] + recv_b[n]

    hand_on(0)
    for c in range(CHUNKS - 1):
        hand_on(c + 1)
        normalize(c)
        for n in range(tiles):
            project(c, n)
    normalize(CHUNKS - 1)
    for n in range(tiles):
        project(CHUNKS - 1, n)
        if n == 0:
            first_copies.extend(give_owners(part.at[0], first_recv, first_sem.at[0], first_sem.at[1]))
        else:
            give_mate(n)
        if n > 3:
            pass_on(n - 3)
    for n in range(tiles - 3, tiles):
        pass_on(n)

    heads_in_tile = TILE // HEAD_WIDTH
    keyval = finish(0)
    mix_copies = []
    key_head = value_head = None
    for t in range(query_tiles):
        if t * heads_in_tile % group_width == 0:
            j = t * heads_in_tile // group_width
            key_head = rotated(keyval[:, 2 * j * HEAD_WIDTH : (2 * j + 1) * HEAD_WIDTH])
            value_head = keyval[:, (2 * j + 1) * HEAD_WIDTH : (2 * j + 2) * HEAD_WIDTH].astype(
                jnp.bfloat16
            )
        query_tile = finish(1 + t)
        query = jnp.concatenate(
            [
                rotated(query_tile[:, h * HEAD_WIDTH : (h + 1) * HEAD_WIDTH])
                for h in range(heads_in_tile)
            ],
            axis=0,
        )
        scores = lax.dot_general(
            query, key_head, (((1,), (1,)), ((), ())), preferred_element_type=jnp.float32
        ) * (HEAD_WIDTH ** (-0.5))
        scores = jnp.where(visible_all, scores, MASK_VALUE)
        weights = jnp.exp(scores - jnp.max(scores, axis=1, keepdims=True))
        probs = (weights / jnp.sum(weights, axis=1, keepdims=True)).astype(jnp.bfloat16)
        mixed = jnp.dot(probs, value_head, preferred_element_type=jnp.float32).astype(jnp.bfloat16)
        for h in range(heads_in_tile):
            mixed_send[t, :, h * HEAD_WIDTH : (h + 1) * HEAD_WIDTH] = mixed[
                h * rows : (h + 1) * rows
            ]

        @pl.when(gx == gy)
        def _():
            mixed_all[t, gy] = mixed_send[t]

        for step in (3, 2, 1, 0):
            copy = pltpu.make_async_remote_copy(
                src_ref=mixed_send.at[t], dst_ref=mixed_all.at[t, gy],
                send_sem=mix_send.at[t, step], recv_sem=mix_recv.at[t, gy],
                device_id={"gx": (gx + step) % side, "gy": gx}, device_id_type=MESH,
            )
            if step == 0:
                pl.when(gx != gy)(copy.start)
            else:
                copy.start()
            mix_copies.append((step, copy))

    def wait_mixed(t):
        for step in range(side):
            r = (gy + step) % side
            copy = pltpu.make_async_remote_copy(
                src_ref=mixed_send.at[t], dst_ref=mixed_all.at[t, r],
                send_sem=mix_send.at[t, 0], recv_sem=mix_recv.at[t, r],
                device_id=mate, device_id_type=MESH,
            )
            if step == 0:
                pl.when(gx != gy)(copy.wait_recv)
            else:
                copy.wait_recv()

    out_tiles = wo_ref.shape[1] // TILE

    def out_term(t, n):
        return jnp.dot(
            mixed_all[t].reshape(side * rows, TILE),
            wo[t * TILE : (t + 1) * TILE, n * TILE : (n + 1) * TILE],
            preferred_element_type=jnp.float32,
        )

    for t in range(query_tiles - 1):
        wait_mixed(t)
        if t == 0:
            weight_copies[2 * CHUNKS].wait()
        if t == query_tiles // 2:
            weight_copies[2 * CHUNKS + 1].wait()
        for n in range(out_tiles):
            out_acc[n] = out_term(t, n) if t == 0 else out_acc[n] + out_term(t, n)
    wait_mixed(query_tiles - 1)

    oa_copies, ob_copies, out_first_copies = [], [], []

    def out_project(n):
        value = out_acc[n] + out_term(query_tiles - 1, n)
        for r in range(side):
            out_part[n, r % 2, r // 2] = value[r * rows : (r + 1) * rows]
        if n == 0:
            out_first_copies.extend(
                give_owners(out_part.at[0], out_first_recv, out_first_sem.at[0], out_first_sem.at[1])
            )
            oa_copies.append(None)
            ob_copies.append(None)
            return
        copy = pltpu.make_async_remote_copy(
            src_ref=out_part.at[n, 1 - core], dst_ref=out_recv_a.at[n],
            send_sem=oa_send.at[n], recv_sem=oa_recv.at[n], device_id=mate, device_id_type=MESH,
        )
        copy.start()
        oa_copies.append(copy)

    def out_pass_on(n):
        oa_copies[n].wait_recv()
        out_sum_b[n] = out_part[n, core, 1 - chip] + out_recv_a[n, 1 - chip]
        copy = pltpu.make_async_remote_copy(
            src_ref=out_sum_b.at[n], dst_ref=out_recv_b.at[n],
            send_sem=ob_send.at[n], recv_sem=ob_recv.at[n], device_id=across, device_id_type=MESH,
        )
        copy.start()
        ob_copies.append(copy)

    for n in range(out_tiles):
        out_project(n)
        if n > 2:
            out_pass_on(n - 2)
    for n in range(out_tiles - 2, out_tiles):
        out_pass_on(n)
    for copy in out_first_copies:
        copy.wait_recv()
    out_ref[:, 0:TILE] = (
        out_part[0, core, chip] + out_first_recv[0] + (out_first_recv[1] + out_first_recv[2])
    ).astype(jnp.bfloat16)
    for n in range(1, out_tiles):
        ob_copies[n].wait_recv()
        out_ref[:, n * TILE : (n + 1) * TILE] = (
            out_part[n, core, chip] + out_recv_a[n, chip] + out_recv_b[n]
        ).astype(jnp.bfloat16)

    for c in range(CHUNKS):
        token_copy(c, 0, gx, outer).wait_send()
        token_copy(c, 1, gx, outer).wait_send()

        @pl.when(middle)
        def _():
            token_copy(c, 2, gx, outer).wait_send()
            token_copy(c, 3, far, outer).wait_send()

    for copy in stat_copies + first_copies + a_copies[1:] + b_copies[1:]:
        copy.wait_send()
    for copy in out_first_copies + oa_copies[1:] + ob_copies[1:]:
        copy.wait_send()
    for step, copy in mix_copies:
        if step == 0:
            pl.when(gx != gy)(copy.wait_send)
        else:
            copy.wait_send()


def fused_on_device(tokens, norm_gain, w_query, keyvalue_weight, w_out, segment_ids):
    rows, width = tokens.shape
    side = lax.axis_size("gx")
    query_tiles = w_query.shape[1] // TILE
    tiles = query_tiles + 1
    out_tiles = w_out.shape[1] // TILE
    f32, bf16 = jnp.float32, jnp.bfloat16
    dma = pltpu.SemaphoreType.DMA
    vmem = pl.BlockSpec(memory_space=pltpu.VMEM)
    hbm = pl.BlockSpec(memory_space=pl.ANY)
    return pl.pallas_call(
        fused_kernel,
        out_shape=jax.ShapeDtypeStruct((rows, w_out.shape[1]), bf16),
        in_specs=[hbm] * 6,
        out_specs=vmem,
        scratch_shapes=[
            pltpu.VMEM((1, width), f32),
            pltpu.VMEM(segment_ids.shape, jnp.int32),
            pltpu.VMEM((CHUNKS, side, rows, width // CHUNKS), bf16),
            pltpu.VMEM((side * side, 2, 128), f32),
            pltpu.VMEM((CHUNKS, side, rows, width // CHUNKS), bf16),
            pltpu.VMEM(w_query.shape, bf16),
            pltpu.VMEM(keyvalue_weight.shape, bf16),
            pltpu.VMEM(w_out.shape, bf16),
            pltpu.VMEM((tiles, 2, 2, rows, TILE), f32),
            pltpu.VMEM((tiles, 2, rows, TILE), f32),
            pltpu.VMEM((tiles, rows, TILE), f32),
            pltpu.VMEM((tiles, rows, TILE), f32),
            pltpu.VMEM((tiles, rows, TILE), f32),
            pltpu.VMEM((query_tiles, rows, TILE), bf16),
            pltpu.VMEM((query_tiles, side, rows, TILE), bf16),
            pltpu.VMEM((out_tiles, side * rows, TILE), f32),
            pltpu.VMEM((out_tiles, 2, 2, rows, TILE), f32),
            pltpu.VMEM((out_tiles, 2, rows, TILE), f32),
            pltpu.VMEM((out_tiles, rows, TILE), f32),
            pltpu.VMEM((out_tiles, rows, TILE), f32),
            pltpu.VMEM((3, rows, TILE), f32),
            dma((2, 3)),
            pltpu.VMEM((3, rows, TILE), f32),
            dma((2, 3)),
            dma((2 + CHUNKS,)), dma((2 * CHUNKS + 2,)),
            dma((CHUNKS, side)), dma((CHUNKS, side)),
            dma((side * side - 1,)), dma((side * side - 1,)),
            dma((tiles,)), dma((tiles,)), dma((tiles,)), dma((tiles,)),
            dma((query_tiles, side)), dma((query_tiles, side)),
            dma((out_tiles,)), dma((out_tiles,)), dma((out_tiles,)), dma((out_tiles,)),
        ],
        compiler_params=pltpu.CompilerParams(
            collective_id=0, has_side_effects=True, vmem_limit_bytes=63 * 1024 * 1024
        ),
        cost_estimate=pl.CostEstimate(
            flops=2 * side * rows * width * (w_query.shape[1] * 2 + keyvalue_weight.shape[1]),
            bytes_accessed=2 * (w_query.size + keyvalue_weight.size + w_out.size),
            transcendentals=0,
        ),
    )(tokens, norm_gain[None, :], segment_ids, w_query, keyvalue_weight, w_out)


def program_for(mesh):
    if mesh.shape["gx"] == 4 and mesh.shape["gy"] == 4:
        return fused_on_device
    return on_device


def solution(mesh):
    return jax.shard_map(
        program_for(mesh),
        mesh=mesh,
        in_specs=(
            P(("groups", "gx"), "gy"),
            P("gy"),
            P("gy", "gx"),
            P("gy", "gx"),
            P("gy", "gx"),
            P(("groups", "gx"), None),
        ),
        out_specs=P(("groups", "gy"), "gx"),
        check_vma=False,
    )
```
